128 devices in a mesh: tm: 8 (over y, core), space: 16 (over x, z).
Axes of the slice: x: 4, y: 4, z: 4, core: 2. Of those that a mesh axis runs over, the one named last changes fastest.
Arguments:
- queries: bfloat16 [16384, 6144], P(('tm', 'space')), may hold values from -5 to 5
- key_rows: bfloat16 [16384, 6144], P(('tm', 'space')), may hold values from -5 to 5
- value_rows: bfloat16 [16384, 6144], P(('tm', 'space')), may hold values from -6 to 6
- tile_lists: int32 [8, 32, 2], P('tm'), may hold values from 0 to 31, as said below
- span_reach: int32 [8, 32], P('tm'), may hold values from 0 to 7, as said below
Outputs:
- attended: bfloat16 [16384, 6144], P(('tm', 'space'))
The draws below stay inside these ranges and needn't reach their ends.
Inputs may be any that keep to these rules, and one draw needn't show every extreme that they name: Each row of tile_lists holds 2 different tiles and begins with the query tile itself. span_reach[c, t] <= c for every span c and tile t; in the last span, tile 0 reaches span 0 and tile 1 reaches only its own span.
All inputs are finite; a program needn't handle non-finite values.
Results may differ from the reference program's by a relative error of at most 0.009.
Values may be sent and summed in bfloat16 or wider, within the bound.
A program may use at most 192 MiB of HBM per device.

```python
import jax
import jax.numpy as jnp

D = 6144
HEADS = 48
DH = 128
TILE = 64
KT = 2
SPANS = 8
CT = 2048
TILES = 32
TOKENS = 16384


def draw_queries(key, part):
    key = jax.random.fold_in(key, 1)
    base = jnp.clip(jax.random.normal(key, (TOKENS, D), jnp.float32), -5.0, 5.0)
    return base.astype(jnp.bfloat16)


def draw_key_rows(key, part):
    key = jax.random.fold_in(key, 2)
    base = jnp.clip(jax.random.normal(key, (TOKENS, D), jnp.float32), -5.0, 5.0)
    return base.astype(jnp.bfloat16)


def draw_span_reach(key, part):
    key = jax.random.fold_in(key, 3)
    spans = jnp.arange(SPANS, dtype=jnp.int32)[:, None]
    tiles = jnp.arange(TILES, dtype=jnp.int32)[None, :]
    raw = jax.random.randint(key, (SPANS, TILES), 0, 2 ** 20, dtype=jnp.int32)
    reach = raw % (spans + 1)
    last = spans == SPANS - 1
    reach = jnp.where(jnp.logical_and(last, tiles == 0), 0, reach)
    reach = jnp.where(jnp.logical_and(last, tiles == 1), SPANS - 1, reach)
    return reach.astype(jnp.int32)


def draw_tile_lists(key, part):
    key = jax.random.fold_in(key, 5)
    raw = jax.random.randint(key, (SPANS, TILES, TILES), 0, 2 ** 20, dtype=jnp.int32)
    tiles = jnp.arange(TILES, dtype=jnp.int32)
    scores = raw * TILES + tiles[None, None, :]
    scores = jnp.where(tiles[None, :, None] == tiles[None, None, :], -1, scores)
    order = jnp.argsort(scores, axis=-1, stable=True)
    return order[:, :, :KT].astype(jnp.int32)


def block_scale(own_key, dims, split, low, top_value):
    def one(position, shards_of):
        draws = jax.random.uniform(jax.random.fold_in(jax.random.fold_in(own_key, 6), position), (shards_of,), jnp.float32, low / len(split), top_value / len(split))
        return jnp.repeat(jnp.exp(draws), dims[position] // shards_of).reshape((-1,) + (1,) * (len(dims) - position - 1))

    level = one(*split[0])
    for cut in split[1:]:
        level = level * one(*cut)
    return level


def normal_values(rng, dims, deviation, most, cuts=(), held_as=jnp.bfloat16):
    loudness = block_scale(rng, dims, cuts, -0.22, 0.18) if cuts else 1.0
    array = jax.random.normal(rng, dims, jnp.float32) * deviation * loudness
    return jnp.minimum(jnp.maximum(array, -most), most).astype(held_as)


def setup_inputs(seed: int = 0) -> dict:
    key_list = jax.random.split(jax.random.key(seed), 6)
    queries = draw_queries(jax.random.fold_in(key_list[5], 71), 0)
    key_rows = draw_key_rows(jax.random.fold_in(key_list[5], 71), 0)
    value_rows = normal_values(key_list[2], (TOKENS, D), 1.0, 6.0, ((0, 128),))
    tile_lists = draw_tile_lists(jax.random.fold_in(key_list[5], 71), 0)
    span_reach = draw_span_reach(jax.random.fold_in(key_list[5], 71), 0)
    return dict(queries=queries, key_rows=key_rows, value_rows=value_rows, tile_lists=tile_lists, span_reach=span_reach)


def span_tiles(rows, span):
    return rows[span * CT:(span + 1) * CT].reshape(TILES, TILE, HEADS, DH)


def reference(queries, key_rows, value_rows, tile_lists, span_reach):
    scale = DH ** -0.5
    results = []
    for span in range(SPANS):
        query_tiles = span_tiles(queries, span).astype(jnp.float32)
        lists = tile_lists[span]
        tops, totals, partials, valids = [], [], [], []
        for source in range(span + 1):
            key_sel = span_tiles(key_rows, source)[lists].reshape(TILES, KT * TILE, HEADS, DH).astype(jnp.float32)
            value_sel = span_tiles(value_rows, source)[lists].reshape(TILES, KT * TILE, HEADS, DH).astype(jnp.float32)
            scores = jnp.einsum('tqhd,tkhd->thqk', query_tiles, key_sel) * scale
            top = jnp.max(scores, axis=-1)
            expo = jnp.exp(scores - top[..., None])
            total = jnp.sum(expo, axis=-1)
            weights = expo.astype(jnp.bfloat16).astype(jnp.float32)
            partial_value = jnp.einsum('thqk,tkhd->thqd', weights, value_sel)
            valid = (source >= span_reach[span])[:, None, None]
            tops.append(jnp.where(valid, top, jnp.float32(-1e30)))
            totals.append(total)
            partials.append(partial_value)
            valids.append(valid)
        big = tops[0]
        for top in tops[1:]:
            big = jnp.maximum(big, top)
        numer = jnp.zeros_like(partials[0])
        denom = jnp.zeros_like(totals[0])
        for top, total, partial_value, valid in zip(tops, totals, partials, valids):
            factor = jnp.where(valid, jnp.exp(top - big), jnp.float32(0.0))
            numer = numer + factor[..., None] * partial_value
            denom = denom + factor * total
        output = numer / denom[..., None]
        results.append(jnp.transpose(output, (0, 2, 1, 3)).reshape(CT, D).astype(jnp.bfloat16))
    return jnp.concatenate(results, axis=0)
```

```python
import functools
import math

import jax
import jax.numpy as jnp
from jax import lax
from jax.experimental import pallas as pl
from jax.experimental.pallas import tpu as pltpu
from jax.sharding import PartitionSpec as P

MESH = pl.DeviceIdType.MESH
DH = 128
TILE = 64
SIDE = 4
CHIPS = 64
HEADS = 48
SPANS = 8
TILES = 32
NEG = -1e30


def offset(i):
    v = (33 * i) % CHIPS
    a, b, c = v % 4, (v // 4) % 4, v // 16
    return (3 * a) % 4, (3 * b + c) % 4, (3 * c) % 4


def kernel(
    q_in, k_in, v_in, meta_in, out, qbuf, kbuf, vbuf, obuf, meta_v, meta_s,
    q_send, k_send, v_send, o_send, m_send, q_recv, k_recv, v_recv, o_recv, m_recv,
    fk_send, fk_recv, fv_send, fv_recv, m_copy,
):
    tm = lax.axis_index("tm")
    sp = lax.axis_index("space")
    y, core = tm // 2, tm % 2
    x, z = sp // SIDE, sp % SIDE
    here = lax.rem(y + SIDE - lax.rem(x + z, SIDE) + 3, SIDE)
    active = here < 3
    sibling = (tm + 1 - 2 * core, sp)

    def chip(i, sign):
        dx, dz, dy = offset(i)
        cx = lax.rem(x + SIDE + sign * dx, SIDE)
        cz = lax.rem(z + SIDE + sign * dz, SIDE)
        cy = lax.rem(y + SIDE + sign * dy, SIDE)
        return cx, cz, cy

    barrier = pltpu.get_barrier_semaphore()

    def greet(i, carry):
        cx, cz, cy = chip(i, 1)
        pl.semaphore_signal(
            barrier, inc=1, device_id=(2 * cy + core, cx * SIDE + cz), device_id_type=MESH
        )
        return carry

    lax.fori_loop(1, CHIPS, greet, 0)
    pl.semaphore_signal(barrier, inc=1, device_id=sibling, device_id_type=MESH)
    pl.semaphore_wait(barrier, CHIPS)

    for d in range(1, SIDE):
        pltpu.make_async_remote_copy(
            meta_in, meta_v.at[y], m_send, m_recv,
            device_id=(2 * lax.rem(y + d, SIDE) + core, sp), device_id_type=MESH,
        ).start()
    pltpu.make_async_copy(meta_in, meta_v.at[y], m_recv).start()

    def send(src, dst, send_sem, recv_sem):
        def one(i, carry):
            cx, cz, cy = chip(i, 1)
            k = lax.rem(cy + SIDE - lax.rem(cx + cz, SIDE) + 3, SIDE)
            head = 3 * (cx * SIDE + cz) + k
            piece = src.at[:, :, pl.ds(pl.multiple_of(head * DH, DH), DH)]

            @pl.when(jnp.logical_and(k < 3, i == 0))
            def _():
                pltpu.make_async_copy(piece, dst(i), recv_sem(i)).start()

            @pl.when(jnp.logical_and(k < 3, i > 0))
            def _():
                pltpu.make_async_remote_copy(
                    piece, dst(i), send_sem, recv_sem(i),
                    device_id=(2 * cy + core, cx * SIDE + cz), device_id_type=MESH,
                ).start()

            return carry

        lax.fori_loop(0, CHIPS, one, 0)

    own = pl.ds(2 * sp, 2)
    send(k_in, lambda i: kbuf.at[own, tm], k_send, lambda i: k_recv.at[y])
    send(v_in, lambda i: vbuf.at[own, tm], v_send, lambda i: v_recv.at[y])
    send(q_in, lambda i: qbuf.at[i], q_send, lambda i: q_recv.at[i])

    pltpu.make_async_copy(meta_v, meta_v, m_recv).wait()
    move = pltpu.make_async_copy(meta_v, meta_s, m_copy)
    move.start()
    move.wait()

    @pl.when(active)
    def _():
        for buf, recv, f_send, f_recv in (
            (kbuf, k_recv, fk_send, fk_recv), (vbuf, v_recv, fv_send, fv_recv),
        ):
            for j in range(SIDE):
                half = buf.at[:, 2 * j + core]
                pltpu.make_async_copy(half, half, recv.at[j]).wait()
                pltpu.make_async_remote_copy(
                    half, half, f_send.at[j], f_recv.at[j],
                    device_id=sibling, device_id_type=MESH,
                ).start()
        for buf, f_recv in ((kbuf, fk_recv), (vbuf, fv_recv)):
            for j in range(SIDE):
                half = buf.at[:, 2 * j + 1 - core]
                pltpu.make_async_copy(half, half, f_recv.at[j]).wait()

        scale = DH ** -0.5 * math.log2(math.e)
        my_head = 3 * sp + here

        def attend(i, j, pair):
            width = 2 * (j + 1)
            keys = width * TILE
            for half in range(2):
                t = 2 * pair + half
                other = meta_s[j, 0, t]
                reach = meta_s[j, 1, t]
                q = qbuf[i, half]
                span = lax.broadcasted_iota(jnp.int32, (1, keys), 1) // TILE
                valid = jnp.logical_and(span >= reach, span <= 2 * j + core)
                bias = jnp.where(valid, 0.0, NEG)
                nt = (((1,), (1,)), ((), ()))
                k_own = kbuf[t, :width].reshape(keys, DH)
                k_other = kbuf[other, :width].reshape(keys, DH)
                s_own = lax.dot_general(q, k_own, nt, preferred_element_type=jnp.float32) + bias
                s_other = lax.dot_general(q, k_other, nt, preferred_element_type=jnp.float32) + bias
                top = jnp.max(jnp.maximum(s_own, s_other), axis=1, keepdims=True)
                e_own = jnp.exp2((s_own - top) * scale)
                e_other = jnp.exp2((s_other - top) * scale)
                total = jnp.sum(e_own + e_other, axis=1, keepdims=True)
                v_own = vbuf[t, :width].reshape(keys, DH)
                v_other = vbuf[other, :width].reshape(keys, DH)
                numer = jnp.dot(
                    e_own.astype(jnp.bfloat16), v_own, preferred_element_type=jnp.float32
                ) + jnp.dot(
                    e_other.astype(jnp.bfloat16), v_other, preferred_element_type=jnp.float32
                )
                obuf[i, half] = (numer / total).astype(jnp.bfloat16)

        def work(i, carry):
            cx, cz, cy = chip(i, -1)
            pair = cx * SIDE + cz
            pltpu.make_async_copy(qbuf.at[i], qbuf.at[i], q_recv.at[i]).wait()
            for j in range(SIDE):
                pl.when(cy == j)(functools.partial(attend, i, j, pair))
            home = out.at[:, :, pl.ds(pl.multiple_of(my_head * DH, DH), DH)]

            @pl.when(i == 0)
            def _():
                pltpu.make_async_copy(obuf.at[i], home, o_recv).start()

            @pl.when(i > 0)
            def _():
                pltpu.make_async_remote_copy(
                    obuf.at[i], home, o_send, o_recv,
                    device_id=(2 * cy + core, pair), device_id_type=MESH,
                ).start()

            return carry

        lax.fori_loop(0, CHIPS, work, 0)

        sent = obuf.at[pl.ds(1, CHIPS - 1)]
        pltpu.make_async_copy(sent, sent, o_send).wait()
        for buf, f_send in ((kbuf, fk_send), (vbuf, fv_send)):
            for j in range(SIDE):
                half = buf.at[:, 2 * j + core]
                pltpu.make_async_copy(half, half, f_send.at[j]).wait()

    for src, sem in ((q_in, q_send), (k_in, k_send), (v_in, v_send)):
        rest = src.at[:, :, pl.ds(0, (HEADS - 1) * DH)]
        pltpu.make_async_copy(rest, rest, sem).wait()

        @pl.when(jnp.logical_not(active))
        def _():
            last = src.at[:, :, pl.ds((HEADS - 1) * DH, DH)]
            pltpu.make_async_copy(last, last, sem).wait()

    lists = meta_v.at[pl.ds(0, SIDE - 1)]
    pltpu.make_async_copy(lists, lists, m_send).wait()
    pltpu.make_async_copy(out, out, o_recv).wait()


def body(queries, key_rows, value_rows, tile_lists, span_reach):
    rows, width = queries.shape
    halves = (rows // TILE, TILE, width)
    meta = jnp.concatenate([tile_lists[0, :, 1][None], span_reach], axis=0)
    meta = jnp.pad(meta, ((0, 6), (0, 128 - TILES)))
    dma = pltpu.SemaphoreType.DMA
    half_work = 2 * SPANS // 2 * TILES // 2 * 64 * 128 * 128 * 5 * 4
    out = pl.pallas_call(
        kernel,
        out_shape=jax.ShapeDtypeStruct(halves, queries.dtype),
        in_specs=[pl.BlockSpec(memory_space=pl.ANY)] * 4,
        out_specs=pl.BlockSpec(memory_space=pl.ANY),
        scratch_shapes=[
            pltpu.VMEM((CHIPS, 2, TILE, DH), jnp.bfloat16),
            pltpu.VMEM((TILES, SPANS, TILE, DH), jnp.bfloat16),
            pltpu.VMEM((TILES, SPANS, TILE, DH), jnp.bfloat16),
            pltpu.VMEM((CHIPS, 2, TILE, DH), jnp.bfloat16),
            pltpu.VMEM((SIDE, 8, 128), jnp.int32),
            pltpu.SMEM((SIDE, 8, 128), jnp.int32),
            dma, dma, dma, dma, dma,
            dma((CHIPS,)), dma((SIDE,)), dma((SIDE,)), dma, dma,
            dma((SIDE,)), dma((SIDE,)), dma((SIDE,)), dma((SIDE,)), dma,
        ],
        compiler_params=pltpu.CompilerParams(
            collective_id=0, has_side_effects=True, vmem_limit_bytes=48 << 20
        ),
        cost_estimate=pl.CostEstimate(
            flops=half_work, bytes_accessed=4 * rows * width * 2, transcendentals=half_work // 512
        ),
        name="attend",
    )(
        queries.reshape(halves), key_rows.reshape(halves), value_rows.reshape(halves), meta
    )
    return out.reshape(rows, width)


def solution(mesh):
    in_specs = (
        P(("tm", "space"), None),
        P(("tm", "space"), None),
        P(("tm", "space"), None),
        P("tm", None, None),
        P("tm", None),
    )
    return jax.shard_map(
        body, mesh=mesh, in_specs=in_specs, out_specs=P(("tm", "space"), None), check_vma=False
    )
```

```python
import math

import jax
import jax.numpy as jnp
from jax import lax
from jax.experimental import pallas as pl
from jax.experimental.pallas import tpu as pltpu
from jax.sharding import PartitionSpec as P

MESH = pl.DeviceIdType.MESH
DH = 128
TILE = 64
SIDE = 4
PLANE = SIDE * SIDE
HEADS = 48
GROUP = 3
TILES = 32
PIECES = PLANE * GROUP
NEG = -1e30
SCALE = DH ** -0.5 * math.log2(math.e)
NT = (((1,), (1,)), ((), ()))


def kernel(
    q_in, k_in, v_in, meta_in, out,
    qbuf, kbuf, vbuf, obuf, lbuf, pbuf, plog, own_o, own_l, meta_v, meta_s,
    q_send, k_send, v_send, o_send, p_send, l_send, m_send,
    q_recv, k_recv, v_recv, o_recv, p_recv, l_recv, m_recv,
    fk_send, fk_recv, fv_send, fv_recv, fq_send, m_copy,
):
    tm = lax.axis_index("tm")
    sp = lax.axis_index("space")
    y, core = tm // 2, tm % 2
    x, z = sp // SIDE, sp % SIDE
    late = y == GROUP
    early = y < GROUP
    sibling = (tm + 1 - 2 * core, sp)

    def place(i, sign):
        a, b = i % SIDE, (i // SIDE) % SIDE
        dx, dz = a, (2 * a + b) % SIDE
        return lax.rem(x + SIDE + sign * dx, SIDE) * SIDE + lax.rem(z + SIDE + sign * dz, SIDE)

    def ring(s):
        return lax.rem(y + s, GROUP)

    def wait(ref, sem):
        pltpu.make_async_copy(ref, ref, sem).wait()

    def columns(head):
        return pl.ds(pl.multiple_of(head * DH, DH), DH)

    barrier = pltpu.get_barrier_semaphore()

    def greet(i, carry):
        where = place(i, 1)
        for d in range(SIDE):
            there = 2 * lax.rem(y + d, SIDE) + core

            @pl.when(jnp.logical_or(i > 0, d > 0))
            def _():
                pl.semaphore_signal(
                    barrier, inc=1, device_id=(there, where), device_id_type=MESH
                )

        return carry

    lax.fori_loop(0, PLANE, greet, 0)
    pl.semaphore_signal(barrier, inc=1, device_id=sibling, device_id_type=MESH)
    pl.semaphore_wait(barrier, PLANE * SIDE)

    for d in range(1, SIDE):
        pltpu.make_async_remote_copy(
            meta_in, meta_v.at[y], m_send, m_recv,
            device_id=(2 * lax.rem(y + d, SIDE) + core, sp), device_id_type=MESH,
        ).start()
    pltpu.make_async_copy(meta_in, meta_v.at[y], m_recv).start()

    def send(src, dst, send_sem, recv_sem):
        def one(i, carry):
            s = lax.rem(i, GROUP)
            where = place(i, 1)
            there = jnp.where(late, GROUP, ring(s))
            head = GROUP * where + jnp.where(late, s, there)
            slot = jnp.where(late, s, y)
            piece = src.at[:, :, columns(head)]
            mine = jnp.logical_and(
                lax.rem(i, PLANE) == 0, jnp.logical_or(late, s == 0)
            )

            @pl.when(mine)
            def _():
                pltpu.make_async_copy(piece, dst(i, slot), recv_sem(i, slot)).start()

            @pl.when(jnp.logical_not(mine))
            def _():
                pltpu.make_async_remote_copy(
                    piece, dst(i, slot), send_sem, recv_sem(i, slot),
                    device_id=(2 * there + core, where), device_id_type=MESH,
                ).start()

            return carry

        lax.fori_loop(0, PIECES, one, 0)

    own = pl.ds(2 * sp, 2)
    send(k_in, lambda i, j: kbuf.at[own, 2 * j + core], k_send, lambda i, j: k_recv.at[j])
    send(v_in, lambda i, j: vbuf.at[own, 2 * j + core], v_send, lambda i, j: v_recv.at[j])
    send(q_in, lambda i, j: qbuf.at[i], q_send, lambda i, j: q_recv.at[i])

    wait(meta_v, m_recv)
    move = pltpu.make_async_copy(meta_v, meta_s, m_copy)
    move.start()
    move.wait()

    swaps = (
        (kbuf, k_recv, fk_send, fk_recv), (vbuf, v_recv, fv_send, fv_recv),
    )
    for buf, recv, f_send, f_recv in swaps:
        for j in range(GROUP):
            half = buf.at[:, 2 * j + core]
            wait(half, recv.at[j])
            pltpu.make_async_remote_copy(
                half, half, f_send.at[j], f_recv.at[j],
                device_id=sibling, device_id_type=MESH,
            ).start()
    for buf, _, _, f_recv in swaps:
        for j in range(GROUP):
            wait(buf.at[:, 2 * j + 1 - core], f_recv.at[j])

    def attend(q, t, other, first, width, valid):
        keys = width * TILE
        spans = pl.ds(first, width)
        bias = jnp.where(valid, 0.0, NEG)
        k = jnp.concatenate(
            [kbuf[t, spans].reshape(keys, DH), kbuf[other, spans].reshape(keys, DH)], axis=0
        )
        s = lax.dot_general(q, k, NT, preferred_element_type=jnp.float32)
        s = s + jnp.concatenate([bias, bias], axis=1)
        top = jnp.max(s, axis=1, keepdims=True)
        e = jnp.exp2((s - top) * SCALE).astype(jnp.bfloat16)
        v = jnp.concatenate(
            [vbuf[t, spans].reshape(keys, DH), vbuf[other, spans].reshape(keys, DH)], axis=0
        )
        v = jnp.concatenate([v, jnp.ones_like(v)], axis=1)
        r = jnp.dot(e, v, preferred_element_type=jnp.float32)
        total = r[:, DH:]
        return r[:, :DH] / total, top * SCALE + jnp.log2(total)

    def spans_of(width, first):
        return first + lax.broadcasted_iota(jnp.int32, (1, width * TILE), 1) // TILE

    def diagonal(half):
        shape = (TILE, DH)
        row = lax.broadcasted_iota(jnp.int32, shape, 0)
        lane = lax.broadcasted_iota(jnp.int32, shape, 1)
        return jnp.where(lane == row + half * TILE, 1.0, 0.0)

    @pl.when(early)
    def _():
        my_head = GROUP * sp + y
        home = out.at[:, :, columns(my_head)]

        def work(n, carry):
            items = []
            for j in range(GROUP):
                i = GROUP * n + lax.rem(y - j + GROUP, GROUP)
                items.append((i, place(i, -1)))
            items.append((PIECES + n, place(GROUP * n + y, -1)))
            for i, _ in items:
                wait(qbuf.at[i], q_recv.at[i])
            logs = []
            for j, (i, where) in enumerate(items):
                width = min(2 * (j + 1), 2 * GROUP)
                span = spans_of(width, 0)
                for half in range(2):
                    t = 2 * where + half
                    valid = span >= meta_s[j, 1, t]
                    if j < GROUP:
                        valid = jnp.logical_and(valid, span <= 2 * j + core)
                    o, log = attend(qbuf[i, half], t, meta_s[j, 0, t], 0, width, valid)
                    obuf[i, half] = o.astype(jnp.bfloat16)
                    if j == GROUP:
                        logs.append(jnp.sum(log * diagonal(half), axis=0, keepdims=True))
            lbuf[n] = jnp.broadcast_to(logs[0] + logs[1], (8, DH))
            for j, (i, where) in enumerate(items[:GROUP]):
                mine = jnp.logical_and(lax.rem(i, PLANE) == 0, j == y)

                @pl.when(mine)
                def _():
                    pltpu.make_async_copy(obuf.at[i], home, o_recv).start()

                @pl.when(jnp.logical_not(mine))
                def _():
                    pltpu.make_async_remote_copy(
                        obuf.at[i], home, o_send, o_recv,
                        device_id=(2 * j + core, where), device_id_type=MESH,
                    ).start()

            i = PIECES + n
            piece = GROUP * n + y
            above = dict(device_id=(2 * GROUP + core, sp), device_id_type=MESH)
            pltpu.make_async_remote_copy(
                obuf.at[i], pbuf.at[piece], p_send, p_recv.at[piece], **above
            ).start()
            pltpu.make_async_remote_copy(
                lbuf.at[n], plog.at[piece], l_send, l_recv.at[piece], **above
            ).start()
            return carry

        lax.fori_loop(0, PLANE, work, 0)
        wait(obuf.at[pl.ds(0, PIECES - 1)], o_send)
        wait(obuf.at[pl.ds(PIECES, PLANE)], p_send)
        wait(lbuf, l_send)

    @pl.when(late)
    def _():
        def work(n, carry):
            for h in range(GROUP):
                i = GROUP * n + h
                wait(qbuf.at[i], q_recv.at[i])
                pltpu.make_async_remote_copy(
                    qbuf.at[i], qbuf.at[PIECES + n], fq_send, q_recv.at[PIECES + n],
                    device_id=(2 * h + core, sp), device_id_type=MESH,
                ).start()
            span = spans_of(2, 2 * GROUP)
            for h in range(GROUP):
                i = GROUP * n + h
                where = place(i, -1)
                for half in range(2):
                    t = 2 * where + half
                    valid = jnp.logical_and(
                        span >= meta_s[GROUP, 1, t], span <= 2 * GROUP + core
                    )
                    o, log = attend(qbuf[i, half], t, meta_s[GROUP, 0, t], 2 * h, 2, valid)
                    own_o[i, half] = o
                    own_l[i, half] = log
            return carry

        lax.fori_loop(0, PLANE, work, 0)

        def merge(i, carry):
            wait(pbuf.at[i], p_recv.at[i])
            wait(plog.at[i], l_recv.at[i])
            where = place(i, -1)
            row = plog[i, 0:1]
            for half in range(2):
                log_b = jnp.sum(row * diagonal(half), axis=1, keepdims=True)
                log_a = own_l[i, half]
                big = jnp.maximum(log_a, log_b)
                factor_a = jnp.exp2(log_a - big)
                factor_b = jnp.exp2(log_b - big)
                numer = factor_a * own_o[i, half] + factor_b * pbuf[i, half].astype(jnp.float32)
                obuf[i, half] = (numer / (factor_a + factor_b)).astype(jnp.bfloat16)
            home = out.at[:, :, columns(GROUP * sp + lax.rem(i, GROUP))]
            mine = lax.rem(i, PLANE) == 0

            @pl.when(mine)
            def _():
                pltpu.make_async_copy(obuf.at[i], home, o_recv).start()

            @pl.when(jnp.logical_not(mine))
            def _():
                pltpu.make_async_remote_copy(
                    obuf.at[i], home, o_send, o_recv,
                    device_id=(2 * GROUP + core, where), device_id_type=MESH,
                ).start()

            return carry

        lax.fori_loop(0, PIECES, merge, 0)
        wait(obuf.at[pl.ds(0, PIECES - GROUP)], o_send)
        wait(qbuf.at[pl.ds(0, PIECES)], fq_send)

    for buf, _, f_send, _ in swaps:
        for j in range(GROUP):
            wait(buf.at[:, 2 * j + core], f_send.at[j])
    for src, sem in ((q_in, q_send), (k_in, k_send), (v_in, v_send)):
        wait(src.at[:, :, pl.ds(0, (PIECES - GROUP) * DH)], sem)

        @pl.when(early)
        def _():
            wait(src.at[:, :, pl.ds(0, (GROUP - 1) * DH)], sem)

    wait(meta_v.at[pl.ds(0, SIDE - 1)], m_send)
    wait(out, o_recv)


def body(queries, key_rows, value_rows, tile_lists, span_reach):
    rows, width = queries.shape
    halves = (rows // TILE, TILE, width)
    meta = jnp.concatenate([tile_lists[0, :, 1][None], span_reach], axis=0)
    meta = jnp.pad(meta, ((0, 6), (0, 128 - TILES)))
    dma = pltpu.SemaphoreType.DMA
    flops = 2 * 2 * 20 * TILES * TILE * 128 * DH
    out = pl.pallas_call(
        kernel,
        out_shape=jax.ShapeDtypeStruct(halves, queries.dtype),
        in_specs=[pl.BlockSpec(memory_space=pl.ANY)] * 4,
        out_specs=pl.BlockSpec(memory_space=pl.ANY),
        scratch_shapes=[
            pltpu.VMEM((PIECES + PLANE, 2, TILE, DH), jnp.bfloat16),
            pltpu.VMEM((TILES, 2 * GROUP, TILE, DH), jnp.bfloat16),
            pltpu.VMEM((TILES, 2 * GROUP, TILE, DH), jnp.bfloat16),
            pltpu.VMEM((PIECES + PLANE, 2, TILE, DH), jnp.bfloat16),
            pltpu.VMEM((PLANE, 8, DH), jnp.float32),
            pltpu.VMEM((PIECES, 2, TILE, DH), jnp.bfloat16),
            pltpu.VMEM((PIECES, 8, DH), jnp.float32),
            pltpu.VMEM((PIECES, 2, TILE, DH), jnp.float32),
            pltpu.VMEM((PIECES, 2, TILE, DH), jnp.float32),
            pltpu.VMEM((SIDE, 8, 128), jnp.int32),
            pltpu.SMEM((SIDE, 8, 128), jnp.int32),
            dma, dma, dma, dma, dma, dma, dma,
            dma((PIECES + PLANE,)), dma((GROUP,)), dma((GROUP,)), dma,
            dma((PIECES,)), dma((PIECES,)), dma,
            dma((GROUP,)), dma((GROUP,)), dma((GROUP,)), dma((GROUP,)), dma, dma,
        ],
        compiler_params=pltpu.CompilerParams(
            collective_id=0, has_side_effects=True, vmem_limit_bytes=60 << 20
        ),
        cost_estimate=pl.CostEstimate(
            flops=flops, bytes_accessed=4 * rows * width * 2, transcendentals=flops // 512
        ),
        name="attend",
    )(
        queries.reshape(halves), key_rows.reshape(halves), value_rows.reshape(halves), meta
    )
    return out.reshape(rows, width)


def solution(mesh):
    in_specs = (
        P(("tm", "space"), None),
        P(("tm", "space"), None),
        P(("tm", "space"), None),
        P("tm", None, None),
        P("tm", None),
    )
    return jax.shard_map(
        body, mesh=mesh, in_specs=in_specs, out_specs=P(("tm", "space"), None), check_vma=False
    )
```

```python
import math

import jax
import jax.numpy as jnp
from jax import lax
from jax.experimental import pallas as pl
from jax.experimental.pallas import tpu as pltpu
from jax.sharding import PartitionSpec as P

MESH = pl.DeviceIdType.MESH
DH = 128
TILE = 64
SIDE = 4
PLANE = SIDE * SIDE
HEADS = 48
GROUP = 3
TILES = 32
PIECES = PLANE * GROUP
NEG = -1e30
SCALE = DH ** -0.5 * math.log2(math.e)
NT = (((1,), (1,)), ((), ()))


def kernel(
    q_in, k_in, v_in, meta_in, out,
    qbuf, kbuf, vbuf, obuf, lbuf, pbuf, plog, own_o, own_l, kpass, vpass, meta_v, meta_s,
    q_send, k_send, v_send, o_send, p_send, l_send, m_send,
    q_recv, k_recv, v_recv, o_recv, p_recv, l_recv, m_recv,
    fk_send, fk_recv, fv_send, fv_recv, fq_send, m_copy, kp_send, kp_recv, vp_send, vp_recv,
):
    tm = lax.axis_index("tm")
    sp = lax.axis_index("space")
    y, core = tm // 2, tm % 2
    x, z = sp // SIDE, sp % SIDE
    late = y == GROUP
    early = y < GROUP
    sibling = (tm + 1 - 2 * core, sp)

    def place(i, sign):
        a, b = i % SIDE, (i // SIDE) % SIDE
        dx, dz = a, (2 * a + b) % SIDE
        return lax.rem(x + SIDE + sign * dx, SIDE) * SIDE + lax.rem(z + SIDE + sign * dz, SIDE)

    def ring(s):
        return lax.rem(y + s, GROUP)

    def wait(ref, sem):
        pltpu.make_async_copy(ref, ref, sem).wait()

    def columns(head):
        return pl.ds(pl.multiple_of(head * DH, DH), DH)

    barrier = pltpu.get_barrier_semaphore()

    def greet(i, carry):
        where = place(i, 1)
        for d in range(SIDE):
            there = 2 * lax.rem(y + d, SIDE) + core

            @pl.when(jnp.logical_or(i > 0, d > 0))
            def _():
                pl.semaphore_signal(
                    barrier, inc=1, device_id=(there, where), device_id_type=MESH
                )

        return carry

    lax.fori_loop(0, PLANE, greet, 0)
    pl.semaphore_signal(barrier, inc=1, device_id=sibling, device_id_type=MESH)
    pl.semaphore_wait(barrier, PLANE * SIDE)

    for d in range(1, SIDE):
        pltpu.make_async_remote_copy(
            meta_in, meta_v.at[y], m_send, m_recv,
            device_id=(2 * lax.rem(y + d, SIDE) + core, sp), device_id_type=MESH,
        ).start()
    pltpu.make_async_copy(meta_in, meta_v.at[y], m_recv).start()

    def send(src, dst, send_sem, recv_sem, by_way=None):
        def one(i, carry):
            s = lax.rem(i, GROUP)
            where = place(i, 1)
            there = jnp.where(late, GROUP, ring(s))
            head = GROUP * where + jnp.where(late, s, there)
            slot = jnp.where(late, s, y)
            piece = src.at[:, :, columns(head)]
            mine = jnp.logical_and(
                lax.rem(i, PLANE) == 0, jnp.logical_or(late, s == 0)
            )

            @pl.when(mine)
            def _():
                pltpu.make_async_copy(piece, dst(i, slot), recv_sem(i, slot)).start()

            turn = jnp.logical_and(y == 0, s == 2) if by_way else False

            @pl.when(jnp.logical_not(jnp.logical_or(mine, turn)))
            def _():
                pltpu.make_async_remote_copy(
                    piece, dst(i, slot), send_sem, recv_sem(i, slot),
                    device_id=(2 * there + core, where), device_id_type=MESH,
                ).start()

            if by_way:
                pass_buf, pass_recv = by_way

                @pl.when(turn)
                def _():
                    n = i // GROUP
                    pltpu.make_async_remote_copy(
                        piece, pass_buf.at[n], send_sem, pass_recv.at[n],
                        device_id=(2 * GROUP + core, where // SIDE * SIDE + z),
                        device_id_type=MESH,
                    ).start()

            return carry

        lax.fori_loop(0, PIECES, one, 0)

    own = pl.ds(2 * sp, 2)
    send(k_in, lambda i, j: kbuf.at[own, 2 * j + core], k_send, lambda i, j: k_recv.at[j], (kpass, kp_recv))
    send(v_in, lambda i, j: vbuf.at[own, 2 * j + core], v_send, lambda i, j: v_recv.at[j], (vpass, vp_recv))
    send(q_in, lambda i, j: qbuf.at[i], q_send, lambda i, j: q_recv.at[i])

    wait(meta_v, m_recv)
    move = pltpu.make_async_copy(meta_v, meta_s, m_copy)
    move.start()
    move.wait()

    passes = (
        (kpass, kp_send, kp_recv, kbuf, k_recv), (vpass, vp_send, vp_recv, vbuf, v_recv),
    )

    @pl.when(late)
    def _():
        for pass_buf, pass_send, pass_recv, buf, recv in passes:
            def onward(n, carry):
                i = GROUP * n + 2
                wait(pass_buf.at[n], pass_recv.at[n])
                source = place(i, -1) // SIDE * SIDE + z
                target = x * SIDE + place(i, 1) % SIDE
                pltpu.make_async_remote_copy(
                    pass_buf.at[n], buf.at[pl.ds(2 * source, 2), core], pass_send, recv.at[0],
                    device_id=(2 * 2 + core, target), device_id_type=MESH,
                ).start()
                return carry

            lax.fori_loop(0, PLANE, onward, 0)

    swaps = (
        (kbuf, k_recv, fk_send, fk_recv), (vbuf, v_recv, fv_send, fv_recv),
    )
    for buf, recv, f_send, f_recv in swaps:
        for j in range(GROUP):
            half = buf.at[:, 2 * j + core]
            wait(half, recv.at[j])
            pltpu.make_async_remote_copy(
                half, half, f_send.at[j], f_recv.at[j],
                device_id=sibling, device_id_type=MESH,
            ).start()
    for buf, _, _, f_recv in swaps:
        for j in range(GROUP):
            wait(buf.at[:, 2 * j + 1 - core], f_recv.at[j])

    def attend(tasks):
        def rows(buf, t, other, first, width):
            spans, keys = pl.ds(first, width), width * TILE
            return jnp.concatenate(
                [buf[t, spans].reshape(keys, DH), buf[other, spans].reshape(keys, DH)], axis=0
            )

        scores = []
        for q, t, other, first, width, valid in tasks:
            bias = jnp.where(valid, 0.0, NEG)
            s = lax.dot_general(
                q, rows(kbuf, t, other, first, width), NT, preferred_element_type=jnp.float32
            )
            scores.append(s + jnp.concatenate([bias, bias], axis=1))
        tops = [jnp.max(s, axis=1, keepdims=True) for s in scores]
        weights = [
            jnp.exp2((s - top) * SCALE).astype(jnp.bfloat16) for s, top in zip(scores, tops)
        ]
        sums = []
        for e, (_, t, other, first, width, _) in zip(weights, tasks):
            v = rows(vbuf, t, other, first, width)
            v = jnp.concatenate([v, jnp.ones_like(v)], axis=1)
            sums.append(jnp.dot(e, v, preferred_element_type=jnp.float32))
        return [
            (r[:, :DH] / r[:, DH:], lambda r=r, top=top: top * SCALE + jnp.log2(r[:, DH:]))
            for r, top in zip(sums, tops)
        ]

    def spans_of(width, first):
        return first + lax.broadcasted_iota(jnp.int32, (1, width * TILE), 1) // TILE

    def diagonal(half):
        shape = (TILE, DH)
        row = lax.broadcasted_iota(jnp.int32, shape, 0)
        lane = lax.broadcasted_iota(jnp.int32, shape, 1)
        return jnp.where(lane == row + half * TILE, 1.0, 0.0)

    @pl.when(early)
    def _():
        my_head = GROUP * sp + y
        home = out.at[:, :, columns(my_head)]

        def work(n, carry):
            items = []
            for j in range(GROUP):
                i = GROUP * n + lax.rem(y - j + GROUP, GROUP)
                items.append((i, place(i, -1)))
            items.append((PIECES + n, place(GROUP * n + y, -1)))
            for i, _ in items:
                wait(qbuf.at[i], q_recv.at[i])
            tasks = []
            for j, (i, where) in enumerate(items):
                width = min(2 * (j + 1), 2 * GROUP)
                span = spans_of(width, 0)
                for half in range(2):
                    t = 2 * where + half
                    valid = span >= meta_s[j, 1, t]
                    if j < GROUP:
                        valid = jnp.logical_and(valid, span <= 2 * j + core)
                    tasks.append((qbuf[i, half], t, meta_s[j, 0, t], 0, width, valid))
            logs = []
            for task, (o, log) in enumerate(attend(tasks)):
                j, half = task // 2, task % 2
                obuf[items[j][0], half] = o.astype(jnp.bfloat16)
                if j == GROUP:
                    logs.append(jnp.sum(log() * diagonal(half), axis=0, keepdims=True))
            lbuf[n] = jnp.broadcast_to(logs[0] + logs[1], (8, DH))
            for j, (i, where) in enumerate(items[:GROUP]):
                mine = jnp.logical_and(lax.rem(i, PLANE) == 0, j == y)

                @pl.when(mine)
                def _():
                    pltpu.make_async_copy(obuf.at[i], home, o_recv).start()

                @pl.when(jnp.logical_not(mine))
                def _():
                    pltpu.make_async_remote_copy(
                        obuf.at[i], home, o_send, o_recv,
                        device_id=(2 * j + core, where), device_id_type=MESH,
                    ).start()

            i = PIECES + n
            piece = GROUP * n + y
            above = dict(device_id=(2 * GROUP + core, sp), device_id_type=MESH)
            pltpu.make_async_remote_copy(
                obuf.at[i], pbuf.at[piece], p_send, p_recv.at[piece], **above
            ).start()
            pltpu.make_async_remote_copy(
                lbuf.at[n], plog.at[piece], l_send, l_recv.at[piece], **above
            ).start()
            return carry

        lax.fori_loop(0, PLANE, work, 0)
        wait(obuf.at[pl.ds(0, PIECES - 1)], o_send)
        wait(obuf.at[pl.ds(PIECES, PLANE)], p_send)
        wait(lbuf, l_send)

    @pl.when(late)
    def _():
        def work(n, carry):
            for h in range(GROUP):
                i = GROUP * n + h
                wait(qbuf.at[i], q_recv.at[i])
                pltpu.make_async_remote_copy(
                    qbuf.at[i], qbuf.at[PIECES + n], fq_send, q_recv.at[PIECES + n],
                    device_id=(2 * h + core, sp), device_id_type=MESH,
                ).start()
            span = spans_of(2, 2 * GROUP)
            tasks = []
            for h in range(GROUP):
                i = GROUP * n + h
                where = place(i, -1)
                for half in range(2):
                    t = 2 * where + half
                    valid = jnp.logical_and(
                        span >= meta_s[GROUP, 1, t], span <= 2 * GROUP + core
                    )
                    tasks.append((qbuf[i, half], t, meta_s[GROUP, 0, t], 2 * h, 2, valid))
            for task, (o, log) in enumerate(attend(tasks)):
                i, half = GROUP * n + task // 2, task % 2
                own_o[i, half] = o
                own_l[i, half] = log()
            return carry

        lax.fori_loop(0, PLANE, work, 0)

        def merge(i, carry):
            wait(pbuf.at[i], p_recv.at[i])
            wait(plog.at[i], l_recv.at[i])
            where = place(i, -1)
            row = plog[i, 0:1]
            for half in range(2):
                log_b = jnp.sum(row * diagonal(half), axis=1, keepdims=True)
                log_a = own_l[i, half]
                big = jnp.maximum(log_a, log_b)
                factor_a = jnp.exp2(log_a - big)
                factor_b = jnp.exp2(log_b - big)
                numer = factor_a * own_o[i, half] + factor_b * pbuf[i, half].astype(jnp.float32)
                obuf[i, half] = (numer / (factor_a + factor_b)).astype(jnp.bfloat16)
            home = out.at[:, :, columns(GROUP * sp + lax.rem(i, GROUP))]
            mine = lax.rem(i, PLANE) == 0

            @pl.when(mine)
            def _():
                pltpu.make_async_copy(obuf.at[i], home, o_recv).start()

            @pl.when(jnp.logical_not(mine))
            def _():
                pltpu.make_async_remote_copy(
                    obuf.at[i], home, o_send, o_recv,
                    device_id=(2 * GROUP + core, where), device_id_type=MESH,
                ).start()

            return carry

        lax.fori_loop(0, PIECES, merge, 0)
        wait(obuf.at[pl.ds(0, PIECES - GROUP)], o_send)
        wait(qbuf.at[pl.ds(0, PIECES)], fq_send)
        for pass_buf, pass_send, _, _, _ in passes:
            wait(pass_buf, pass_send)

    for buf, _, f_send, _ in swaps:
        for j in range(GROUP):
            wait(buf.at[:, 2 * j + core], f_send.at[j])
    for src, sem in ((q_in, q_send), (k_in, k_send), (v_in, v_send)):
        wait(src.at[:, :, pl.ds(0, (PIECES - GROUP) * DH)], sem)

        @pl.when(early)
        def _():
            wait(src.at[:, :, pl.ds(0, (GROUP - 1) * DH)], sem)

    wait(meta_v.at[pl.ds(0, SIDE - 1)], m_send)
    wait(out, o_recv)


def body(queries, key_rows, value_rows, tile_lists, span_reach):
    rows, width = queries.shape
    halves = (rows // TILE, TILE, width)
    meta = jnp.concatenate([tile_lists[0, :, 1][None], span_reach], axis=0)
    meta = jnp.pad(meta, ((0, 6), (0, 128 - TILES)))
    dma = pltpu.SemaphoreType.DMA
    flops = 2 * 2 * 20 * TILES * TILE * 128 * DH
    out = pl.pallas_call(
        kernel,
        out_shape=jax.ShapeDtypeStruct(halves, queries.dtype),
        in_specs=[pl.BlockSpec(memory_space=pltpu.HBM)] * 3 + [pl.BlockSpec(memory_space=pl.ANY)],
        out_specs=pl.BlockSpec(memory_space=pl.ANY),
        scratch_shapes=[
            pltpu.VMEM((PIECES + PLANE, 2, TILE, DH), jnp.bfloat16),
            pltpu.VMEM((TILES, 2 * GROUP, TILE, DH), jnp.bfloat16),
            pltpu.VMEM((TILES, 2 * GROUP, TILE, DH), jnp.bfloat16),
            pltpu.VMEM((PIECES + PLANE, 2, TILE, DH), jnp.bfloat16),
            pltpu.VMEM((PLANE, 8, DH), jnp.float32),
            pltpu.VMEM((PIECES, 2, TILE, DH), jnp.bfloat16),
            pltpu.VMEM((PIECES, 8, DH), jnp.float32),
            pltpu.VMEM((PIECES, 2, TILE, DH), jnp.float32),
            pltpu.VMEM((PIECES, 2, TILE, DH), jnp.float32),
            pltpu.VMEM((PLANE, 2, TILE, DH), jnp.bfloat16),
            pltpu.VMEM((PLANE, 2, TILE, DH), jnp.bfloat16),
            pltpu.VMEM((SIDE, 8, 128), jnp.int32),
            pltpu.SMEM((SIDE, 8, 128), jnp.int32),
            dma, dma, dma, dma, dma, dma, dma,
            dma((PIECES + PLANE,)), dma((GROUP,)), dma((GROUP,)), dma,
            dma((PIECES,)), dma((PIECES,)), dma,
            dma((GROUP,)), dma((GROUP,)), dma((GROUP,)), dma((GROUP,)), dma, dma,
            dma, dma((PLANE,)), dma, dma((PLANE,)),
        ],
        compiler_params=pltpu.CompilerParams(
            collective_id=0, has_side_effects=True, vmem_limit_bytes=60 << 20
        ),
        cost_estimate=pl.CostEstimate(
            flops=flops, bytes_accessed=4 * rows * width * 2, transcendentals=flops // 512
        ),
        name="attend",
    )(
        queries.reshape(halves), key_rows.reshape(halves), value_rows.reshape(halves), meta
    )
    return out.reshape(rows, width)


def solution(mesh):
    in_specs = (
        P(("tm", "space"), None),
        P(("tm", "space"), None),
        P(("tm", "space"), None),
        P("tm", None, None),
        P("tm", None),
    )
    return jax.shard_map(
        body, mesh=mesh, in_specs=in_specs, out_specs=P(("tm", "space"), None), check_vma=False
    )
```

```python
import math

import jax
import jax.numpy as jnp
from jax import lax
from jax.experimental import pallas as pl
from jax.experimental.pallas import tpu as pltpu
from jax.sharding import PartitionSpec as P

MESH = pl.DeviceIdType.MESH
DH = 128
TILE = 64
SIDE = 4
PLANE = SIDE * SIDE
HEADS = 48
GROUP = 3
TILES = 32
PIECES = PLANE * GROUP
BATCH = 4
NEG = -1e30
SCALE = DH ** -0.5 * math.log2(math.e)
NT = (((1,), (1,)), ((), ()))


def kernel(
    q_in, k_in, v_in, lists_in, reach_in, out,
    qbuf, kbuf, vbuf, obuf, lbuf, pbuf, plog, vpass, qpass, lists_v, reach_v, lists_s, reach_s,
    q_send, k_send, v_send, o_send, p_send, l_send, m_send,
    q_recv, k_recv, v_recv, o_recv, p_recv, l_recv, m_recv,
    fk_send, fk_recv, fv_send, fv_recv, fq_send, m_copy, vp_send, vp_recv, qp_send, qp_recv,
):
    tm = lax.axis_index("tm")
    sp = lax.axis_index("space")
    y, core = tm // 2, tm % 2
    x, z = sp // SIDE, sp % SIDE
    late = y == GROUP
    early = y < GROUP
    sibling = (tm + 1 - 2 * core, sp)

    def place(i, sign):
        a, b = i % SIDE, (i // SIDE) % SIDE
        dx, dz = a, (2 * a + b) % SIDE
        return lax.rem(x + SIDE + sign * dx, SIDE) * SIDE + lax.rem(z + SIDE + sign * dz, SIDE)

    def ring(s):
        return lax.rem(y + s, GROUP)

    def wait(ref, sem):
        pltpu.make_async_copy(ref, ref, sem).wait()

    def columns(head):
        return pl.ds(pl.multiple_of(head * DH, DH), DH)

    barrier = pltpu.get_barrier_semaphore()

    def greet(i, carry):
        where = place(i, 1)
        for d in range(SIDE):
            there = 2 * lax.rem(y + d, SIDE) + core

            @pl.when(jnp.logical_or(i > 0, d > 0))
            def _():
                pl.semaphore_signal(
                    barrier, inc=1, device_id=(there, where), device_id_type=MESH
                )

        return carry

    lax.fori_loop(0, PLANE, greet, 0)
    pl.semaphore_signal(barrier, inc=1, device_id=sibling, device_id_type=MESH)
    pl.semaphore_wait(barrier, PLANE * SIDE)

    lists = ((lists_in, lists_v, lists_s), (reach_in, reach_v, reach_s))
    for k, (src, dst, _) in enumerate(lists):
        for d in range(1, SIDE):
            pltpu.make_async_remote_copy(
                src, dst.at[y], m_send.at[k], m_recv.at[k],
                device_id=(2 * lax.rem(y + d, SIDE) + core, sp), device_id_type=MESH,
            ).start()
        pltpu.make_async_copy(src, dst.at[y], m_recv.at[k]).start()

    def send(kind, src, dst, send_sem, recv_sem, by_way=None):
        def one(i, carry):
            s = lax.rem(i, GROUP)
            where = place(i, 1)
            there = GROUP if kind == "late" else ring(s)
            head = GROUP * where + (s if kind == "late" else there)
            piece = src.at[:, :, columns(head)]
            mine = lax.rem(i, PLANE) == 0
            if kind == "early":
                mine = jnp.logical_and(mine, s == 0)
            turn = jnp.logical_and(y == 0, s == 2) if by_way else False

            @pl.when(mine)
            def _():
                pltpu.make_async_copy(piece, dst(i), recv_sem.at[i]).start()

            @pl.when(jnp.logical_not(jnp.logical_or(mine, turn)))
            def _():
                pltpu.make_async_remote_copy(
                    piece, dst(i), send_sem, recv_sem.at[i],
                    device_id=(2 * there + core, where), device_id_type=MESH,
                ).start()

            if by_way:
                pass_buf, pass_recv = by_way

                @pl.when(turn)
                def _():
                    n = i // GROUP
                    pltpu.make_async_remote_copy(
                        piece, pass_buf.at[n], send_sem, pass_recv.at[n],
                        device_id=(2 * GROUP + core, where // SIDE * SIDE + z),
                        device_id_type=MESH,
                    ).start()

            return carry

        lax.fori_loop(0, PIECES, one, 0)

    def span_slot(buf, pair, j):
        return buf.at[pl.ds(2 * pair, 2), 2 * j + core]

    def swap(i, j, buf, recv, f_send, f_recv):
        piece = span_slot(buf, place(i, -1), j)
        wait(piece, recv.at[i])
        pltpu.make_async_remote_copy(
            piece, piece, f_send, f_recv, device_id=sibling, device_id_type=MESH
        ).start()

    def onward(n, pass_buf, pass_send, pass_recv, dst, recv):
        i = GROUP * n + 2
        wait(pass_buf.at[n], pass_recv.at[n])
        pltpu.make_async_remote_copy(
            pass_buf.at[n], dst(i), pass_send, recv.at[i],
            device_id=(2 * 2 + core, x * SIDE + place(i, 1) % SIDE), device_id_type=MESH,
        ).start()

    def from_zero(buf):
        return lambda i: span_slot(buf, place(i, -1) // SIDE * SIDE + z, 0)

    swap_k = (kbuf, k_recv, fk_send, fk_recv)
    swap_v = (vbuf, v_recv, fv_send, fv_recv)
    pass_v = (vpass, vp_send, vp_recv, from_zero(vbuf), v_recv)
    pass_q = (qpass, qp_send, qp_recv, lambda i: qbuf.at[i], q_recv)

    def lists_ready():
        for k, (_, buf, _) in enumerate(lists):
            wait(buf, m_recv.at[k])
        moves = [pltpu.make_async_copy(v, s, m_copy.at[k]) for k, (_, v, s) in enumerate(lists)]
        for move in moves:
            move.start()
        for move in moves:
            move.wait()

    def swapped():
        wait(kbuf.at[:, pl.ds(0, GROUP)], fk_recv)
        wait(vbuf.at[:, pl.ds(0, GROUP)], fv_recv)

    @pl.when(early)
    def _():
        send("early", k_in, lambda i: span_slot(kbuf, sp, y), k_send, k_recv)
        send("early", v_in, lambda i: span_slot(vbuf, sp, y), v_send, v_recv, (vpass, vp_recv))
        send("early", q_in, lambda i: qbuf.at[i], q_send, q_recv, (qpass, qp_recv))
        lists_ready()
        for what in (swap_k, swap_v):
            def pieces(i, carry):
                swap(i, lax.rem(y + GROUP - lax.rem(i, GROUP), GROUP), *what)
                return carry

            lax.fori_loop(0, PIECES, pieces, 0)
        swapped()

    @pl.when(late)
    def _():
        send("late", q_in, lambda i: qbuf.at[i], q_send, q_recv)
        send("late", k_in, lambda i: span_slot(kbuf, sp, lax.rem(i, GROUP)), k_send, k_recv)
        send("late", v_in, lambda i: span_slot(vbuf, sp, lax.rem(i, GROUP)), v_send, v_recv)
        lists_ready()

        def first(n, carry):
            for h in range(GROUP):
                i = GROUP * n + h
                wait(qbuf.at[i], q_recv.at[i])
                pltpu.make_async_remote_copy(
                    qbuf.at[i], qbuf.at[PIECES + n], fq_send, q_recv.at[PIECES + n],
                    device_id=(2 * h + core, sp), device_id_type=MESH,
                ).start()
            return carry

        lax.fori_loop(0, PLANE, first, 0)

        def second(n, carry):
            onward(n, *pass_v)
            return carry

        lax.fori_loop(0, PLANE, second, 0)

        def third(i, carry):
            swap(i, lax.rem(i, GROUP), *swap_k)
            return carry

        lax.fori_loop(0, PIECES, third, 0)

        def fourth(n, carry):
            for h in range(GROUP):
                swap(GROUP * n + h, h, *swap_v)
            onward(n, *pass_q)
            return carry

        lax.fori_loop(0, PLANE, fourth, 0)
        swapped()

    def attend(tasks):
        def rows(buf, t, other, first, width):
            spans, keys = pl.ds(first, width), width * TILE
            return jnp.concatenate(
                [buf[t, spans].reshape(keys, DH), buf[other, spans].reshape(keys, DH)], axis=0
            )

        scores = []
        for q, t, other, first, width, valid in tasks:
            bias = jnp.where(valid, 0.0, NEG)
            s = lax.dot_general(
                q, rows(kbuf, t, other, first, width), NT, preferred_element_type=jnp.float32
            )
            scores.append(s + jnp.concatenate([bias, bias], axis=1))
        tops = [jnp.max(s, axis=1, keepdims=True) for s in scores]
        weights = [
            jnp.exp2((s - top) * SCALE).astype(jnp.bfloat16) for s, top in zip(scores, tops)
        ]
        sums = []
        for e, (_, t, other, first, width, _) in zip(weights, tasks):
            v = rows(vbuf, t, other, first, width)
            v = jnp.concatenate([v, jnp.ones_like(v)], axis=1)
            sums.append(jnp.dot(e, v, preferred_element_type=jnp.float32))
        return [
            (r[:, :DH] / r[:, DH:], lambda r=r, top=top: top * SCALE + jnp.log2(r[:, DH:]))
            for r, top in zip(sums, tops)
        ]

    def spans_of(width, first):
        return first + lax.broadcasted_iota(jnp.int32, (1, width * TILE), 1) // TILE

    def diagonal(half):
        shape = (TILE, DH)
        row = lax.broadcasted_iota(jnp.int32, shape, 0)
        lane = lax.broadcasted_iota(jnp.int32, shape, 1)
        return jnp.where(lane == row + half * TILE, 1.0, 0.0)

    @pl.when(early)
    def _():
        home = out.at[:, :, columns(GROUP * sp + y)]

        def task(i, half, j, pair):
            width = min(2 * (j + 1), 2 * GROUP)
            span = spans_of(width, 0)
            t = 2 * pair + half
            valid = span >= reach_s[j, 0, t]
            if j < GROUP:
                valid = jnp.logical_and(valid, span <= 2 * j + core)
            return qbuf[i, half], t, lists_s[j, 1, t], 0, width, valid

        def last_spans(m, carry):
            chunks = [BATCH * m + c for c in range(BATCH)]
            for n in chunks:
                wait(qbuf.at[PIECES + n], q_recv.at[PIECES + n])
            done = attend([
                task(PIECES + n, half, GROUP, place(GROUP * n + y, -1))
                for n in chunks for half in range(2)
            ])
            for c, n in enumerate(chunks):
                log = 0.0
                for half in range(2):
                    o, logs = done[2 * c + half]
                    obuf[PIECES + n, half] = o.astype(jnp.bfloat16)
                    log = log + jnp.sum(logs() * diagonal(half), axis=0, keepdims=True)
                lbuf[n] = jnp.broadcast_to(log, (8, DH))
            for n in chunks:
                piece = GROUP * n + y
                above = dict(device_id=(2 * GROUP + core, sp), device_id_type=MESH)
                pltpu.make_async_remote_copy(
                    obuf.at[PIECES + n], pbuf.at[piece], p_send, p_recv.at[piece], **above
                ).start()
                pltpu.make_async_remote_copy(
                    lbuf.at[n], plog.at[piece], l_send, l_recv.at[piece], **above
                ).start()
            return carry

        lax.fori_loop(0, PLANE // BATCH, last_spans, 0)

        def work(n, carry):
            items = []
            for j in range(GROUP):
                i = GROUP * n + lax.rem(y - j + GROUP, GROUP)
                items.append((i, place(i, -1)))
            for i, _ in items:
                wait(qbuf.at[i], q_recv.at[i])
            done = attend([
                task(i, half, j, pair)
                for j, (i, pair) in enumerate(items) for half in range(2)
            ])
            for j, (i, pair) in enumerate(items):
                for half in range(2):
                    obuf[i, half] = done[2 * j + half][0].astype(jnp.bfloat16)
                mine = jnp.logical_and(lax.rem(i, PLANE) == 0, j == y)

                @pl.when(mine)
                def _():
                    pltpu.make_async_copy(obuf.at[i], home, o_recv).start()

                @pl.when(jnp.logical_not(mine))
                def _():
                    pltpu.make_async_remote_copy(
                        obuf.at[i], home, o_send, o_recv,
                        device_id=(2 * j + core, pair), device_id_type=MESH,
                    ).start()

            return carry

        lax.fori_loop(0, PLANE, work, 0)
        wait(obuf.at[pl.ds(0, PIECES - 1)], o_send)
        wait(obuf.at[pl.ds(PIECES, PLANE)], p_send)
        wait(lbuf, l_send)

    @pl.when(late)
    def _():
        def work(n, carry):
            pieces = [GROUP * n + h for h in range(GROUP)]
            span = spans_of(2, 2 * GROUP)
            tasks = []
            for h, i in enumerate(pieces):
                pair = place(i, -1)
                for half in range(2):
                    t = 2 * pair + half
                    valid = jnp.logical_and(
                        span >= reach_s[GROUP, 0, t], span <= 2 * GROUP + core
                    )
                    tasks.append((qbuf[i, half], t, lists_s[GROUP, 1, t], 2 * h, 2, valid))
            done = attend(tasks)
            for i in pieces:
                wait(pbuf.at[i], p_recv.at[i])
                wait(plog.at[i], l_recv.at[i])
            merged = []
            for k, (o, log) in enumerate(done):
                i, half = pieces[k // 2], k % 2
                log_a = log()
                log_b = jnp.sum(plog[i, 0:1] * diagonal(half), axis=1, keepdims=True)
                big = jnp.maximum(log_a, log_b)
                factor_a = jnp.exp2(log_a - big)
                factor_b = jnp.exp2(log_b - big)
                numer = factor_a * o + factor_b * pbuf[i, half].astype(jnp.float32)
                merged.append((numer / (factor_a + factor_b)).astype(jnp.bfloat16))
            for k, o in enumerate(merged):
                obuf[pieces[k // 2], k % 2] = o
            for h, i in enumerate(pieces):
                home = out.at[:, :, columns(GROUP * sp + h)]
                mine = lax.rem(i, PLANE) == 0

                @pl.when(mine)
                def _():
                    pltpu.make_async_copy(obuf.at[i], home, o_recv).start()

                @pl.when(jnp.logical_not(mine))
                def _():
                    pltpu.make_async_remote_copy(
                        obuf.at[i], home, o_send, o_recv,
                        device_id=(2 * GROUP + core, place(i, -1)), device_id_type=MESH,
                    ).start()

            return carry

        lax.fori_loop(0, PLANE, work, 0)
        wait(obuf.at[pl.ds(0, PIECES - GROUP)], o_send)
        wait(qbuf.at[pl.ds(0, PIECES)], fq_send)
        wait(vpass, vp_send)
        wait(qpass, qp_send)

    wait(kbuf.at[:, pl.ds(0, GROUP)], fk_send)
    wait(vbuf.at[:, pl.ds(0, GROUP)], fv_send)
    for src, sem in ((q_in, q_send), (k_in, k_send), (v_in, v_send)):
        wait(src.at[:, :, pl.ds(0, (PIECES - GROUP) * DH)], sem)

        @pl.when(early)
        def _():
            wait(src.at[:, :, pl.ds(0, (GROUP - 1) * DH)], sem)

    for k, (_, buf, _) in enumerate(lists):
        wait(buf.at[pl.ds(0, SIDE - 1)], m_send.at[k])
    wait(out, o_recv)


def body(queries, key_rows, value_rows, tile_lists, span_reach):
    rows, width = queries.shape
    halves = (rows // TILE, TILE, width)
    dma = pltpu.SemaphoreType.DMA
    flops = 2 * 2 * 20 * TILES * TILE * 128 * DH
    out = pl.pallas_call(
        kernel,
        out_shape=jax.ShapeDtypeStruct(halves, queries.dtype),
        in_specs=[pl.BlockSpec(memory_space=pltpu.HBM)] * 3 + [pl.BlockSpec(memory_space=pl.ANY)] * 2,
        out_specs=pl.BlockSpec(memory_space=pl.ANY),
        scratch_shapes=[
            pltpu.VMEM((PIECES + PLANE, 2, TILE, DH), jnp.bfloat16),
            pltpu.VMEM((TILES, 2 * GROUP, TILE, DH), jnp.bfloat16),
            pltpu.VMEM((TILES, 2 * GROUP, TILE, DH), jnp.bfloat16),
            pltpu.VMEM((PIECES + PLANE, 2, TILE, DH), jnp.bfloat16),
            pltpu.VMEM((PLANE, 8, DH), jnp.float32),
            pltpu.VMEM((PIECES, 2, TILE, DH), jnp.bfloat16),
            pltpu.VMEM((PIECES, 8, DH), jnp.float32),
            pltpu.VMEM((PLANE, 2, TILE, DH), jnp.bfloat16),
            pltpu.VMEM((PLANE, 2, TILE, DH), jnp.bfloat16),
            pltpu.VMEM((SIDE, 2, TILES), jnp.int32),
            pltpu.VMEM((SIDE, 1, TILES), jnp.int32),
            pltpu.SMEM((SIDE, 2, TILES), jnp.int32),
            pltpu.SMEM((SIDE, 1, TILES), jnp.int32),
            dma, dma, dma, dma, dma, dma, dma((2,)),
            dma((PIECES + PLANE,)), dma((PIECES,)), dma((PIECES,)), dma,
            dma((PIECES,)), dma((PIECES,)), dma((2,)),
            dma, dma, dma, dma, dma, dma((2,)),
            dma, dma((PLANE,)), dma, dma((PLANE,)),
        ],
        compiler_params=pltpu.CompilerParams(
            collective_id=0, has_side_effects=True, vmem_limit_bytes=48 << 20
        ),
        cost_estimate=pl.CostEstimate(
            flops=flops, bytes_accessed=4 * rows * width * 2, transcendentals=flops // 512
        ),
        name="attend",
    )(
        *(
            pltpu.with_memory_space_constraint(array, pltpu.HBM)
            for array in (
                queries.reshape(halves), key_rows.reshape(halves), value_rows.reshape(halves),
                tile_lists[0].T, span_reach,
            )
        ),
    )
    return out.reshape(rows, width)


def solution(mesh):
    in_specs = (
        P(("tm", "space"), None),
        P(("tm", "space"), None),
        P(("tm", "space"), None),
        P("tm", None, None),
        P("tm", None),
    )
    return jax.shard_map(
        body, mesh=mesh, in_specs=in_specs, out_specs=P(("tm", "space"), None), check_vma=False
    )
```

```python
import math

import jax
import jax.numpy as jnp
from jax import lax
from jax.experimental import pallas as pl
from jax.experimental.pallas import tpu as pltpu
from jax.sharding import PartitionSpec as P

MESH = pl.DeviceIdType.MESH
DH = 128
TILE = 64
SIDE = 4
PLANE = SIDE * SIDE
HEADS = 48
GROUP = 3
TILES = 32
PIECES = PLANE * GROUP
BATCH = 2
STEP = 2
NEG = -1e30
SCALE = DH ** -0.5 * math.log2(math.e)
NT = (((1,), (1,)), ((), ()))


def kernel(
    q_in, k_in, v_in, lists_in, reach_in, out,
    qbuf, kbuf, vbuf, obuf, lbuf, pbuf, plog, vpass, qpass, lists_v, reach_v, lists_s, reach_s,
    q_send, k_send, v_send, o_send, p_send, l_send, m_send,
    q_recv, k_recv, v_recv, o_recv, p_recv, l_recv, m_recv,
    fk_send, fk_recv, fv_send, fv_recv, fq_send, m_copy, vp_send, vp_recv, qp_send, qp_recv,
):
    tm = lax.axis_index("tm")
    sp = lax.axis_index("space")
    y, core = tm // 2, tm % 2
    x, z = sp // SIDE, sp % SIDE
    late = y == GROUP
    early = y < GROUP
    sibling = (tm + 1 - 2 * core, sp)

    def place(i, sign):
        a, b = i % SIDE, (i // SIDE) % SIDE
        dx, dz = a, (2 * a + b) % SIDE
        return lax.rem(x + SIDE + sign * dx, SIDE) * SIDE + lax.rem(z + SIDE + sign * dz, SIDE)

    def ring(s):
        return lax.rem(y + s, GROUP)

    def wait(ref, sem):
        pltpu.make_async_copy(ref, ref, sem).wait()

    def columns(head):
        return pl.ds(pl.multiple_of(head * DH, DH), DH)

    barrier = pltpu.get_barrier_semaphore()

    for dx in range(SIDE):
        for dz in range(SIDE):
            for dy in range(SIDE):
                if dx or dz or dy:
                    where = lax.rem(x + dx, SIDE) * SIDE + lax.rem(z + dz, SIDE)
                    pl.semaphore_signal(
                        barrier, inc=1, device_id=(2 * lax.rem(y + dy, SIDE) + core, where),
                        device_id_type=MESH,
                    )
    pl.semaphore_signal(barrier, inc=1, device_id=sibling, device_id_type=MESH)
    pl.semaphore_wait(barrier, PLANE * SIDE)

    lists = ((lists_in, lists_v, lists_s), (reach_in, reach_v, reach_s))
    for k, (src, dst, _) in enumerate(lists):
        for d in range(1, SIDE):
            pltpu.make_async_remote_copy(
                src, dst.at[y], m_send.at[k], m_recv.at[k],
                device_id=(2 * lax.rem(y + d, SIDE) + core, sp), device_id_type=MESH,
            ).start()
        pltpu.make_async_copy(src, dst.at[y], m_recv.at[k]).start()

    def send(kind, src, dst, send_sem, recv_sem, by_way=None):
        def one(i, carry):
            s = lax.rem(i, GROUP)
            where = place(i, 1)
            there = GROUP if kind == "late" else ring(s)
            head = GROUP * where + (s if kind == "late" else there)
            piece = src.at[:, :, columns(head)]
            mine = lax.rem(i, PLANE) == 0
            if kind == "early":
                mine = jnp.logical_and(mine, s == 0)
            turn = jnp.logical_and(y == 0, s == 2) if by_way else False

            @pl.when(mine)
            def _():
                pltpu.make_async_copy(piece, dst(i), recv_sem.at[i]).start()

            @pl.when(jnp.logical_not(jnp.logical_or(mine, turn)))
            def _():
                pltpu.make_async_remote_copy(
                    piece, dst(i), send_sem, recv_sem.at[i],
                    device_id=(2 * there + core, where), device_id_type=MESH,
                ).start()

            if by_way:
                pass_buf, pass_recv = by_way

                @pl.when(turn)
                def _():
                    n = i // GROUP
                    pltpu.make_async_remote_copy(
                        piece, pass_buf.at[n], send_sem, pass_recv.at[n],
                        device_id=(2 * GROUP + core, where // SIDE * SIDE + z),
                        device_id_type=MESH,
                    ).start()

            return carry

        lax.fori_loop(0, PIECES, one, 0)

    def span_slot(buf, pair, j):
        return buf.at[pl.ds(2 * pair, 2), 2 * j + core]

    def swap(i, j, buf, recv, f_send, f_recv):
        piece = span_slot(buf, place(i, -1), j)
        wait(piece, recv.at[i])
        pltpu.make_async_remote_copy(
            piece, piece, f_send, f_recv, device_id=sibling, device_id_type=MESH
        ).start()

    def onward(n, pass_buf, pass_send, pass_recv, dst, recv):
        i = GROUP * n + 2
        wait(pass_buf.at[n], pass_recv.at[n])
        pltpu.make_async_remote_copy(
            pass_buf.at[n], dst(i), pass_send, recv.at[i],
            device_id=(2 * 2 + core, x * SIDE + place(i, 1) % SIDE), device_id_type=MESH,
        ).start()

    def from_zero(buf):
        return lambda i: span_slot(buf, place(i, -1) // SIDE * SIDE + z, 0)

    swap_k = (kbuf, k_recv, fk_send, fk_recv)
    swap_v = (vbuf, v_recv, fv_send, fv_recv)
    pass_v = (vpass, vp_send, vp_recv, from_zero(vbuf), v_recv)
    pass_q = (qpass, qp_send, qp_recv, lambda i: qbuf.at[i], q_recv)

    def lists_ready():
        for k, (_, buf, _) in enumerate(lists):
            wait(buf, m_recv.at[k])
        moves = [pltpu.make_async_copy(v, s, m_copy.at[k]) for k, (_, v, s) in enumerate(lists)]
        for move in moves:
            move.start()
        for move in moves:
            move.wait()

    def swapped():
        wait(kbuf.at[:, pl.ds(0, GROUP)], fk_recv)
        wait(vbuf.at[:, pl.ds(0, GROUP)], fv_recv)

    @pl.when(early)
    def _():
        send("early", k_in, lambda i: span_slot(kbuf, sp, y), k_send, k_recv)
        send("early", v_in, lambda i: span_slot(vbuf, sp, y), v_send, v_recv, (vpass, vp_recv))
        send("early", q_in, lambda i: qbuf.at[i], q_send, q_recv, (qpass, qp_recv))
        lists_ready()
        for what in (swap_k, swap_v):
            def pieces(i, carry):
                swap(i, lax.rem(y + GROUP - lax.rem(i, GROUP), GROUP), *what)
                return carry

            lax.fori_loop(0, PIECES, pieces, 0)
        swapped()

    @pl.when(late)
    def _():
        send("late", q_in, lambda i: qbuf.at[i], q_send, q_recv)
        send("late", k_in, lambda i: span_slot(kbuf, sp, lax.rem(i, GROUP)), k_send, k_recv)
        send("late", v_in, lambda i: span_slot(vbuf, sp, lax.rem(i, GROUP)), v_send, v_recv)
        lists_ready()

        def first(n, carry):
            for h in range(GROUP):
                i = GROUP * n + h
                wait(qbuf.at[i], q_recv.at[i])
                pltpu.make_async_remote_copy(
                    qbuf.at[i], qbuf.at[PIECES + n], fq_send, q_recv.at[PIECES + n],
                    device_id=(2 * h + core, sp), device_id_type=MESH,
                ).start()
            return carry

        lax.fori_loop(0, PLANE, first, 0)

        def second(n, carry):
            onward(n, *pass_v)
            return carry

        lax.fori_loop(0, PLANE, second, 0)

        def third(i, carry):
            swap(i, lax.rem(i, GROUP), *swap_k)
            return carry

        lax.fori_loop(0, PIECES, third, 0)

        def fourth(n, carry):
            for h in range(GROUP):
                swap(GROUP * n + h, h, *swap_v)
            onward(n, *pass_q)
            return carry

        lax.fori_loop(0, PLANE, fourth, 0)
        swapped()

    def attend(tasks):
        def rows(buf, t, other, first, width):
            spans, keys = pl.ds(first, width), width * TILE
            return jnp.concatenate(
                [buf[t, spans].reshape(keys, DH), buf[other, spans].reshape(keys, DH)], axis=0
            )

        scores = []
        for q, t, other, first, width, valid in tasks:
            bias = jnp.where(valid, 0.0, NEG)
            s = lax.dot_general(
                q, rows(kbuf, t, other, first, width), NT, preferred_element_type=jnp.float32
            )
            scores.append(s + jnp.concatenate([bias, bias], axis=1))
        tops = [jnp.max(s, axis=1, keepdims=True) for s in scores]
        weights = [jnp.exp2((s - top) * SCALE) for s, top in zip(scores, tops)]
        totals = [jnp.sum(e, axis=1, keepdims=True) for e in weights]
        sums = []
        for e, (_, t, other, first, width, _) in zip(weights, tasks):
            v = rows(vbuf, t, other, first, width)
            sums.append(jnp.dot(e.astype(jnp.bfloat16), v, preferred_element_type=jnp.float32))
        return [
            (r / total, lambda top=top, total=total: top * SCALE + jnp.log2(total))
            for r, top, total in zip(sums, tops, totals)
        ]

    def spans_of(width, first):
        return first + lax.broadcasted_iota(jnp.int32, (1, width * TILE), 1) // TILE

    def diagonal(half):
        shape = (TILE, DH)
        row = lax.broadcasted_iota(jnp.int32, shape, 0)
        lane = lax.broadcasted_iota(jnp.int32, shape, 1)
        return jnp.where(lane == row + half * TILE, 1.0, 0.0)

    @pl.when(early)
    def _():
        home = out.at[:, :, columns(GROUP * sp + y)]

        def task(i, half, j, pair):
            width = min(2 * (j + 1), 2 * GROUP)
            span = spans_of(width, 0)
            t = 2 * pair + half
            valid = span >= reach_s[j, 0, t]
            if j < GROUP:
                valid = jnp.logical_and(valid, span <= 2 * j + core)
            return qbuf[i, half], t, lists_s[j, 1, t], 0, width, valid

        def last_spans(m, carry):
            chunks = [BATCH * m + c for c in range(BATCH)]
            for n in chunks:
                wait(qbuf.at[PIECES + n], q_recv.at[PIECES + n])
            done = attend([
                task(PIECES + n, half, GROUP, place(GROUP * n + y, -1))
                for n in chunks for half in range(2)
            ])
            for c, n in enumerate(chunks):
                log = 0.0
                for half in range(2):
                    o, logs = done[2 * c + half]
                    obuf[PIECES + n, half] = o.astype(jnp.bfloat16)
                    log = log + jnp.sum(logs() * diagonal(half), axis=0, keepdims=True)
                lbuf[n] = jnp.broadcast_to(log, (8, DH))
            for n in chunks:
                piece = GROUP * n + y
                above = dict(device_id=(2 * GROUP + core, sp), device_id_type=MESH)
                pltpu.make_async_remote_copy(
                    obuf.at[PIECES + n], pbuf.at[piece], p_send, p_recv.at[piece], **above
                ).start()
                pltpu.make_async_remote_copy(
                    lbuf.at[n], plog.at[piece], l_send, l_recv.at[piece], **above
                ).start()
            return carry

        def work(m, carry):
            items = []
            for n in [STEP * m + c for c in range(STEP)]:
                for j in range(GROUP):
                    i = GROUP * n + lax.rem(y - j + GROUP, GROUP)
                    items.append((i, j, place(i, -1)))
            for i, _, _ in items:
                wait(qbuf.at[i], q_recv.at[i])
            done = attend([
                task(i, half, j, pair) for i, j, pair in items for half in range(2)
            ])
            for k, (i, j, pair) in enumerate(items):
                for half in range(2):
                    obuf[i, half] = done[2 * k + half][0].astype(jnp.bfloat16)
                mine = jnp.logical_and(lax.rem(i, PLANE) == 0, j == y)

                @pl.when(mine)
                def _():
                    pltpu.make_async_copy(obuf.at[i], home, o_recv).start()

                @pl.when(jnp.logical_not(mine))
                def _():
                    pltpu.make_async_remote_copy(
                        obuf.at[i], home, o_send, o_recv,
                        device_id=(2 * j + core, pair), device_id_type=MESH,
                    ).start()

            return carry

        def both(m, carry):
            last_spans(m + 1, 0)
            work(m, 0)
            return carry

        lax.fori_loop(0, 1, last_spans, 0)
        lax.fori_loop(0, PLANE // BATCH - 1, both, 0)
        lax.fori_loop(PLANE // BATCH - 1, PLANE // STEP, work, 0)
        wait(obuf.at[pl.ds(0, PIECES - 1)], o_send)
        wait(obuf.at[pl.ds(PIECES, PLANE)], p_send)
        wait(lbuf, l_send)

    @pl.when(late)
    def _():
        def work(n, carry):
            pieces = [GROUP * n + h for h in range(GROUP)]
            span = spans_of(2, 2 * GROUP)
            tasks = []
            for h, i in enumerate(pieces):
                pair = place(i, -1)
                for half in range(2):
                    t = 2 * pair + half
                    valid = jnp.logical_and(
                        span >= reach_s[GROUP, 0, t], span <= 2 * GROUP + core
                    )
                    tasks.append((qbuf[i, half], t, lists_s[GROUP, 1, t], 2 * h, 2, valid))
            done = attend(tasks)
            for i in pieces:
                wait(pbuf.at[i], p_recv.at[i])
                wait(plog.at[i], l_recv.at[i])
            merged = []
            for k, (o, log) in enumerate(done):
                i, half = pieces[k // 2], k % 2
                log_a = log()
                log_b = jnp.sum(plog[i, 0:1] * diagonal(half), axis=1, keepdims=True)
                big = jnp.maximum(log_a, log_b)
                factor_a = jnp.exp2(log_a - big)
                factor_b = jnp.exp2(log_b - big)
                numer = factor_a * o + factor_b * pbuf[i, half].astype(jnp.float32)
                merged.append((numer / (factor_a + factor_b)).astype(jnp.bfloat16))
            for k, o in enumerate(merged):
                obuf[pieces[k // 2], k % 2] = o
            for h, i in enumerate(pieces):
                home = out.at[:, :, columns(GROUP * sp + h)]
                mine = lax.rem(i, PLANE) == 0

                @pl.when(mine)
                def _():
                    pltpu.make_async_copy(obuf.at[i], home, o_recv).start()

                @pl.when(jnp.logical_not(mine))
                def _():
                    pltpu.make_async_remote_copy(
                        obuf.at[i], home, o_send, o_recv,
                        device_id=(2 * GROUP + core, place(i, -1)), device_id_type=MESH,
                    ).start()

            return carry

        lax.fori_loop(0, PLANE, work, 0)
        wait(obuf.at[pl.ds(0, PIECES - GROUP)], o_send)
        wait(qbuf.at[pl.ds(0, PIECES)], fq_send)
        wait(vpass, vp_send)
        wait(qpass, qp_send)

    wait(kbuf.at[:, pl.ds(0, GROUP)], fk_send)
    wait(vbuf.at[:, pl.ds(0, GROUP)], fv_send)
    for src, sem in ((q_in, q_send), (k_in, k_send), (v_in, v_send)):
        wait(src.at[:, :, pl.ds(0, (PIECES - GROUP) * DH)], sem)

        @pl.when(early)
        def _():
            wait(src.at[:, :, pl.ds(0, (GROUP - 1) * DH)], sem)

    for k, (_, buf, _) in enumerate(lists):
        wait(buf.at[pl.ds(0, SIDE - 1)], m_send.at[k])
    wait(out, o_recv)


def body(queries, key_rows, value_rows, tile_lists, span_reach):
    rows, width = queries.shape
    halves = (rows // TILE, TILE, width)
    dma = pltpu.SemaphoreType.DMA
    flops = 2 * 2 * 20 * TILES * TILE * 128 * DH
    out = pl.pallas_call(
        kernel,
        out_shape=jax.ShapeDtypeStruct(halves, queries.dtype),
        in_specs=[pl.BlockSpec(memory_space=pltpu.HBM)] * 3 + [pl.BlockSpec(memory_space=pl.ANY)] * 2,
        out_specs=pl.BlockSpec(memory_space=pl.ANY),
        scratch_shapes=[
            pltpu.VMEM((PIECES + PLANE, 2, TILE, DH), jnp.bfloat16),
            pltpu.VMEM((TILES, 2 * GROUP, TILE, DH), jnp.bfloat16),
            pltpu.VMEM((TILES, 2 * GROUP, TILE, DH), jnp.bfloat16),
            pltpu.VMEM((PIECES + PLANE, 2, TILE, DH), jnp.bfloat16),
            pltpu.VMEM((PLANE, 8, DH), jnp.float32),
            pltpu.VMEM((PIECES, 2, TILE, DH), jnp.bfloat16),
            pltpu.VMEM((PIECES, 8, DH), jnp.float32),
            pltpu.VMEM((PLANE, 2, TILE, DH), jnp.bfloat16),
            pltpu.VMEM((PLANE, 2, TILE, DH), jnp.bfloat16),
            pltpu.VMEM((SIDE, 2, TILES), jnp.int32),
            pltpu.VMEM((SIDE, 1, TILES), jnp.int32),
            pltpu.SMEM((SIDE, 2, TILES), jnp.int32),
            pltpu.SMEM((SIDE, 1, TILES), jnp.int32),
            dma, dma, dma, dma, dma, dma, dma((2,)),
            dma((PIECES + PLANE,)), dma((PIECES,)), dma((PIECES,)), dma,
            dma((PIECES,)), dma((PIECES,)), dma((2,)),
            dma, dma, dma, dma, dma, dma((2,)),
            dma, dma((PLANE,)), dma, dma((PLANE,)),
        ],
        compiler_params=pltpu.CompilerParams(
            collective_id=0, has_side_effects=True, vmem_limit_bytes=48 << 20
        ),
        cost_estimate=pl.CostEstimate(
            flops=flops, bytes_accessed=4 * rows * width * 2, transcendentals=flops // 512
        ),
        name="attend",
    )(
        *(
            pltpu.with_memory_space_constraint(array, pltpu.HBM)
            for array in (
                queries.reshape(halves), key_rows.reshape(halves), value_rows.reshape(halves),
                tile_lists[0].T, span_reach,
            )
        ),
    )
    return out.reshape(rows, width)


def solution(mesh):
    in_specs = (
        P(("tm", "space"), None),
        P(("tm", "space"), None),
        P(("tm", "space"), None),
        P("tm", None, None),
        P("tm", None),
    )
    return jax.shard_map(
        body, mesh=mesh, in_specs=in_specs, out_specs=P(("tm", "space"), None), check_vma=False
    )
```

```python
import math

import jax
import jax.numpy as jnp
from jax import lax
from jax.experimental import pallas as pl
from jax.experimental.pallas import tpu as pltpu
from jax.sharding import PartitionSpec as P

MESH = pl.DeviceIdType.MESH
DH = 128
TILE = 64
SIDE = 4
PLANE = SIDE * SIDE
HEADS = 48
GROUP = 3
TILES = 32
PIECES = PLANE * GROUP
BATCH = 2
STEP = 2
NEG = -1e30
SCALE = DH ** -0.5 * math.log2(math.e)
NT = (((1,), (1,)), ((), ()))


def kernel(
    q_in, k_in, v_in, lists_in, reach_in, out,
    qbuf, kbuf, vbuf, obuf, lbuf, pbuf, plog, vpass, qpass, lists_v, reach_v, lists_s, reach_s,
    q_send, k_send, v_send, o_send, p_send, l_send, m_send,
    q_recv, k_recv, v_recv, o_recv, p_recv, l_recv, m_recv,
    fk_send, fk_recv, fv_send, fv_recv, fq_send, m_copy, vp_send, vp_recv, qp_send, qp_recv,
):
    tm = lax.axis_index("tm")
    sp = lax.axis_index("space")
    y, core = tm // 2, tm % 2
    x, z = sp // SIDE, sp % SIDE
    late = y == GROUP
    early = y < GROUP
    sibling = (tm + 1 - 2 * core, sp)

    def place(i, sign):
        a, b = i % SIDE, (i // SIDE) % SIDE
        dx, dz = (2 * a + 3 * b) % SIDE, (3 * a) % SIDE
        return lax.rem(x + SIDE + sign * dx, SIDE) * SIDE + lax.rem(z + SIDE + sign * dz, SIDE)

    def ring(s):
        return lax.rem(y + s, GROUP)

    def wait(ref, sem):
        pltpu.make_async_copy(ref, ref, sem).wait()

    def columns(head):
        return pl.ds(pl.multiple_of(head * DH, DH), DH)

    barrier = pltpu.get_barrier_semaphore()

    for dx in range(SIDE):
        for dz in range(SIDE):
            for dy in range(SIDE):
                if dx or dz or dy:
                    where = lax.rem(x + dx, SIDE) * SIDE + lax.rem(z + dz, SIDE)
                    pl.semaphore_signal(
                        barrier, inc=1, device_id=(2 * lax.rem(y + dy, SIDE) + core, where),
                        device_id_type=MESH,
                    )
    pl.semaphore_signal(barrier, inc=1, device_id=sibling, device_id_type=MESH)
    pl.semaphore_wait(barrier, PLANE * SIDE)

    lists = ((lists_in, lists_v, lists_s), (reach_in, reach_v, reach_s))
    for k, (src, dst, _) in enumerate(lists):
        for d in range(1, SIDE):
            pltpu.make_async_remote_copy(
                src, dst.at[y], m_send.at[k], m_recv.at[k],
                device_id=(2 * lax.rem(y + d, SIDE) + core, sp), device_id_type=MESH,
            ).start()
        pltpu.make_async_copy(src, dst.at[y], m_recv.at[k]).start()

    def send(kind, src, dst, send_sem, recv_sem, by_way=None):
        def one(i, carry):
            s = lax.rem(i, GROUP)
            where = place(i, 1)
            there = GROUP if kind == "late" else ring(s)
            head = GROUP * where + (s if kind == "late" else there)
            piece = src.at[:, :, columns(head)]
            mine = lax.rem(i, PLANE) == 0
            if kind == "early":
                mine = jnp.logical_and(mine, s == 0)
            turn = jnp.logical_and(y == 0, s == 2) if by_way else False

            @pl.when(mine)
            def _():
                pltpu.make_async_copy(piece, dst(i), recv_sem.at[i]).start()

            @pl.when(jnp.logical_not(jnp.logical_or(mine, turn)))
            def _():
                pltpu.make_async_remote_copy(
                    piece, dst(i), send_sem, recv_sem.at[i],
                    device_id=(2 * there + core, where), device_id_type=MESH,
                ).start()

            if by_way:
                pass_buf, pass_recv = by_way

                @pl.when(turn)
                def _():
                    n = i // GROUP
                    pltpu.make_async_remote_copy(
                        piece, pass_buf.at[n], send_sem, pass_recv.at[n],
                        device_id=(2 * GROUP + core, where // SIDE * SIDE + z),
                        device_id_type=MESH,
                    ).start()

            return carry

        lax.fori_loop(0, PIECES, one, 0)

    def span_slot(buf, pair, j):
        return buf.at[pl.ds(2 * pair, 2), 2 * j + core]

    def swap(i, j, buf, recv, f_send, f_recv):
        piece = span_slot(buf, place(i, -1), j)
        wait(piece, recv.at[i])
        pltpu.make_async_remote_copy(
            piece, piece, f_send, f_recv, device_id=sibling, device_id_type=MESH
        ).start()

    def onward(n, pass_buf, pass_send, pass_recv, dst, recv):
        i = GROUP * n + 2
        wait(pass_buf.at[n], pass_recv.at[n])
        pltpu.make_async_remote_copy(
            pass_buf.at[n], dst(i), pass_send, recv.at[i],
            device_id=(2 * 2 + core, x * SIDE + place(i, 1) % SIDE), device_id_type=MESH,
        ).start()

    def from_zero(buf):
        return lambda i: span_slot(buf, place(i, -1) // SIDE * SIDE + z, 0)

    swap_k = (kbuf, k_recv, fk_send, fk_recv)
    swap_v = (vbuf, v_recv, fv_send, fv_recv)
    pass_v = (vpass, vp_send, vp_recv, from_zero(vbuf), v_recv)
    pass_q = (qpass, qp_send, qp_recv, lambda i: qbuf.at[i], q_recv)

    def lists_ready():
        for k, (_, buf, _) in enumerate(lists):
            wait(buf, m_recv.at[k])
        moves = [pltpu.make_async_copy(v, s, m_copy.at[k]) for k, (_, v, s) in enumerate(lists)]
        for move in moves:
            move.start()
        for move in moves:
            move.wait()

    def swapped():
        wait(kbuf.at[:, pl.ds(0, GROUP)], fk_recv)
        wait(vbuf.at[:, pl.ds(0, GROUP)], fv_recv)

    @pl.when(early)
    def _():
        send("early", k_in, lambda i: span_slot(kbuf, sp, y), k_send, k_recv)
        send("early", v_in, lambda i: span_slot(vbuf, sp, y), v_send, v_recv, (vpass, vp_recv))
        send("early", q_in, lambda i: qbuf.at[i], q_send, q_recv, (qpass, qp_recv))
        lists_ready()
        for what in (swap_k, swap_v):
            def pieces(i, carry):
                swap(i, lax.rem(y + GROUP - lax.rem(i, GROUP), GROUP), *what)
                return carry

            lax.fori_loop(0, PIECES, pieces, 0)
        swapped()

    @pl.when(late)
    def _():
        send("late", q_in, lambda i: qbuf.at[i], q_send, q_recv)
        send("late", k_in, lambda i: span_slot(kbuf, sp, lax.rem(i, GROUP)), k_send, k_recv)
        send("late", v_in, lambda i: span_slot(vbuf, sp, lax.rem(i, GROUP)), v_send, v_recv)
        lists_ready()

        def first(n, carry):
            for h in range(GROUP):
                i = GROUP * n + h
                wait(qbuf.at[i], q_recv.at[i])
                pltpu.make_async_remote_copy(
                    qbuf.at[i], qbuf.at[PIECES + n], fq_send, q_recv.at[PIECES + n],
                    device_id=(2 * h + core, sp), device_id_type=MESH,
                ).start()
            return carry

        lax.fori_loop(0, PLANE, first, 0)

        def second(n, carry):
            onward(n, *pass_v)
            return carry

        lax.fori_loop(0, PLANE, second, 0)

        def third(i, carry):
            swap(i, lax.rem(i, GROUP), *swap_k)
            return carry

        lax.fori_loop(0, PIECES, third, 0)

        def fourth(n, carry):
            for h in range(GROUP):
                swap(GROUP * n + h, h, *swap_v)
            onward(n, *pass_q)
            return carry

        lax.fori_loop(0, PLANE, fourth, 0)
        swapped()

    def attend(tasks):
        def rows(buf, t, other, first, width):
            spans, keys = pl.ds(first, width), width * TILE
            return jnp.concatenate(
                [buf[t, spans].reshape(keys, DH), buf[other, spans].reshape(keys, DH)], axis=0
            )

        scores = []
        for q, t, other, first, width, valid in tasks:
            bias = jnp.where(valid, 0.0, NEG)
            s = lax.dot_general(
                q, rows(kbuf, t, other, first, width), NT, preferred_element_type=jnp.float32
            )
            scores.append(s + jnp.concatenate([bias, bias], axis=1))
        tops = [jnp.max(s, axis=1, keepdims=True) for s in scores]
        weights = [jnp.exp2((s - top) * SCALE) for s, top in zip(scores, tops)]
        totals = [jnp.sum(e, axis=1, keepdims=True) for e in weights]
        sums = []
        for e, (_, t, other, first, width, _) in zip(weights, tasks):
            v = rows(vbuf, t, other, first, width)
            sums.append(jnp.dot(e.astype(jnp.bfloat16), v, preferred_element_type=jnp.float32))
        return [
            (r / total, lambda top=top, total=total: top * SCALE + jnp.log2(total))
            for r, top, total in zip(sums, tops, totals)
        ]

    def spans_of(width, first):
        return first + lax.broadcasted_iota(jnp.int32, (1, width * TILE), 1) // TILE

    def diagonal(half):
        shape = (TILE, DH)
        row = lax.broadcasted_iota(jnp.int32, shape, 0)
        lane = lax.broadcasted_iota(jnp.int32, shape, 1)
        return jnp.where(lane == row + half * TILE, 1.0, 0.0)

    @pl.when(early)
    def _():
        home = out.at[:, :, columns(GROUP * sp + y)]

        def task(i, half, j, pair):
            width = min(2 * (j + 1), 2 * GROUP)
            span = spans_of(width, 0)
            t = 2 * pair + half
            valid = span >= reach_s[j, 0, t]
            if j < GROUP:
                valid = jnp.logical_and(valid, span <= 2 * j + core)
            return qbuf[i, half], t, lists_s[j, 1, t], 0, width, valid

        def last_spans(m, carry):
            chunks = [BATCH * m + c for c in range(BATCH)]
            for n in chunks:
                wait(qbuf.at[PIECES + n], q_recv.at[PIECES + n])
            done = attend([
                task(PIECES + n, half, GROUP, place(GROUP * n + y, -1))
                for n in chunks for half in range(2)
            ])
            for c, n in enumerate(chunks):
                log = 0.0
                for half in range(2):
                    o, logs = done[2 * c + half]
                    obuf[PIECES + n, half] = o.astype(jnp.bfloat16)
                    log = log + jnp.sum(logs() * diagonal(half), axis=0, keepdims=True)
                lbuf[n] = jnp.broadcast_to(log, (8, DH))
            for n in chunks:
                piece = GROUP * n + y
                above = dict(device_id=(2 * GROUP + core, sp), device_id_type=MESH)
                pltpu.make_async_remote_copy(
                    obuf.at[PIECES + n], pbuf.at[piece], p_send, p_recv.at[piece], **above
                ).start()
                pltpu.make_async_remote_copy(
                    lbuf.at[n], plog.at[piece], l_send, l_recv.at[piece], **above
                ).start()
            return carry

        def work(m, carry):
            items = []
            for n in [STEP * m + c for c in range(STEP)]:
                for j in range(GROUP):
                    i = GROUP * n + lax.rem(y - j + GROUP, GROUP)
                    items.append((i, j, place(i, -1)))
            for i, _, _ in items:
                wait(qbuf.at[i], q_recv.at[i])
            done = attend([
                task(i, half, j, pair) for i, j, pair in items for half in range(2)
            ])
            for k, (i, j, pair) in enumerate(items):
                for half in range(2):
                    obuf[i, half] = done[2 * k + half][0].astype(jnp.bfloat16)
                mine = jnp.logical_and(lax.rem(i, PLANE) == 0, j == y)

                @pl.when(mine)
                def _():
                    pltpu.make_async_copy(obuf.at[i], home, o_recv).start()

                @pl.when(jnp.logical_not(mine))
                def _():
                    pltpu.make_async_remote_copy(
                        obuf.at[i], home, o_send, o_recv,
                        device_id=(2 * j + core, pair), device_id_type=MESH,
                    ).start()

            return carry

        def both(m, carry):
            last_spans(m + 1, 0)
            work(m, 0)
            return carry

        lax.fori_loop(0, 1, last_spans, 0)
        lax.fori_loop(0, PLANE // BATCH - 1, both, 0)
        lax.fori_loop(PLANE // BATCH - 1, PLANE // STEP, work, 0)
        wait(obuf.at[pl.ds(0, PIECES - 1)], o_send)
        wait(obuf.at[pl.ds(PIECES, PLANE)], p_send)
        wait(lbuf, l_send)

    @pl.when(late)
    def _():
        def work(n, carry):
            pieces = [GROUP * n + h for h in range(GROUP)]
            span = spans_of(2, 2 * GROUP)
            tasks = []
            for h, i in enumerate(pieces):
                pair = place(i, -1)
                for half in range(2):
                    t = 2 * pair + half
                    valid = jnp.logical_and(
                        span >= reach_s[GROUP, 0, t], span <= 2 * GROUP + core
                    )
                    tasks.append((qbuf[i, half], t, lists_s[GROUP, 1, t], 2 * h, 2, valid))
            done = attend(tasks)
            for i in pieces:
                wait(pbuf.at[i], p_recv.at[i])
                wait(plog.at[i], l_recv.at[i])
            merged = []
            for k, (o, log) in enumerate(done):
                i, half = pieces[k // 2], k % 2
                log_a = log()
                log_b = jnp.sum(plog[i, 0:1] * diagonal(half), axis=1, keepdims=True)
                big = jnp.maximum(log_a, log_b)
                factor_a = jnp.exp2(log_a - big)
                factor_b = jnp.exp2(log_b - big)
                numer = factor_a * o + factor_b * pbuf[i, half].astype(jnp.float32)
                merged.append((numer / (factor_a + factor_b)).astype(jnp.bfloat16))
            for k, o in enumerate(merged):
                obuf[pieces[k // 2], k % 2] = o
            for h, i in enumerate(pieces):
                home = out.at[:, :, columns(GROUP * sp + h)]
                mine = lax.rem(i, PLANE) == 0

                @pl.when(mine)
                def _():
                    pltpu.make_async_copy(obuf.at[i], home, o_recv).start()

                @pl.when(jnp.logical_not(mine))
                def _():
                    pltpu.make_async_remote_copy(
                        obuf.at[i], home, o_send, o_recv,
                        device_id=(2 * GROUP + core, place(i, -1)), device_id_type=MESH,
                    ).start()

            return carry

        lax.fori_loop(0, PLANE, work, 0)
        wait(obuf.at[pl.ds(0, PIECES - GROUP)], o_send)
        wait(qbuf.at[pl.ds(0, PIECES)], fq_send)
        wait(vpass, vp_send)
        wait(qpass, qp_send)

    wait(kbuf.at[:, pl.ds(0, GROUP)], fk_send)
    wait(vbuf.at[:, pl.ds(0, GROUP)], fv_send)
    for src, sem in ((q_in, q_send), (k_in, k_send), (v_in, v_send)):
        wait(src.at[:, :, pl.ds(0, (PIECES - GROUP) * DH)], sem)

        @pl.when(early)
        def _():
            wait(src.at[:, :, pl.ds(0, (GROUP - 1) * DH)], sem)

    for k, (_, buf, _) in enumerate(lists):
        wait(buf.at[pl.ds(0, SIDE - 1)], m_send.at[k])
    wait(out, o_recv)


def body(queries, key_rows, value_rows, tile_lists, span_reach):
    rows, width = queries.shape
    halves = (rows // TILE, TILE, width)
    dma = pltpu.SemaphoreType.DMA
    flops = 2 * 2 * 20 * TILES * TILE * 128 * DH
    out = pl.pallas_call(
        kernel,
        out_shape=jax.ShapeDtypeStruct(halves, queries.dtype),
        in_specs=[pl.BlockSpec(memory_space=pltpu.HBM)] * 3 + [pl.BlockSpec(memory_space=pl.ANY)] * 2,
        out_specs=pl.BlockSpec(memory_space=pl.ANY),
        scratch_shapes=[
            pltpu.VMEM((PIECES + PLANE, 2, TILE, DH), jnp.bfloat16),
            pltpu.VMEM((TILES, 2 * GROUP, TILE, DH), jnp.bfloat16),
            pltpu.VMEM((TILES, 2 * GROUP, TILE, DH), jnp.bfloat16),
            pltpu.VMEM((PIECES + PLANE, 2, TILE, DH), jnp.bfloat16),
            pltpu.VMEM((PLANE, 8, DH), jnp.float32),
            pltpu.VMEM((PIECES, 2, TILE, DH), jnp.bfloat16),
            pltpu.VMEM((PIECES, 8, DH), jnp.float32),
            pltpu.VMEM((PLANE, 2, TILE, DH), jnp.bfloat16),
            pltpu.VMEM((PLANE, 2, TILE, DH), jnp.bfloat16),
            pltpu.VMEM((SIDE, 2, TILES), jnp.int32),
            pltpu.VMEM((SIDE, 1, TILES), jnp.int32),
            pltpu.SMEM((SIDE, 2, TILES), jnp.int32),
            pltpu.SMEM((SIDE, 1, TILES), jnp.int32),
            dma, dma, dma, dma, dma, dma, dma((2,)),
            dma((PIECES + PLANE,)), dma((PIECES,)), dma((PIECES,)), dma,
            dma((PIECES,)), dma((PIECES,)), dma((2,)),
            dma, dma, dma, dma, dma, dma((2,)),
            dma, dma((PLANE,)), dma, dma((PLANE,)),
        ],
        compiler_params=pltpu.CompilerParams(
            collective_id=0, has_side_effects=True, vmem_limit_bytes=48 << 20
        ),
        cost_estimate=pl.CostEstimate(
            flops=flops, bytes_accessed=4 * rows * width * 2, transcendentals=flops // 512
        ),
        name="attend",
    )(
        *(
            pltpu.with_memory_space_constraint(array, pltpu.HBM)
            for array in (
                queries.reshape(halves), key_rows.reshape(halves), value_rows.reshape(halves),
                tile_lists[0].T, span_reach,
            )
        ),
    )
    return out.reshape(rows, width)


def solution(mesh):
    in_specs = (
        P(("tm", "space"), None),
        P(("tm", "space"), None),
        P(("tm", "space"), None),
        P("tm", None, None),
        P("tm", None),
    )
    return jax.shard_map(
        body, mesh=mesh, in_specs=in_specs, out_specs=P(("tm", "space"), None), check_vma=False
    )
```

```python
import math

import jax
import jax.numpy as jnp
from jax import lax
from jax.experimental import pallas as pl
from jax.experimental.pallas import tpu as pltpu
from jax.sharding import PartitionSpec as P

MESH = pl.DeviceIdType.MESH
DH = 128
TILE = 64
SIDE = 4
PLANE = SIDE * SIDE
HEADS = 48
GROUP = 3
TILES = 32
PIECES = PLANE * GROUP
BATCH = 2
STEP = 2
NEG = -1e30
SCALE = DH ** -0.5 * math.log2(math.e)
NT = (((1,), (1,)), ((), ()))


def kernel(
    q_in, k_in, v_in, lists_in, reach_in, out,
    qbuf, kbuf, vbuf, obuf, lbuf, pbuf, plog, kpass, qpass, lists_v, reach_v, lists_s, reach_s,
    q_send, k_send, v_send, o_send, p_send, l_send, m_send,
    q_recv, k_recv, v_recv, o_recv, p_recv, l_recv, m_recv,
    fk_send, fk_recv, fv_send, fv_recv, fq_send, m_copy, kp_send, kp_recv, qp_send, qp_recv,
):
    tm = lax.axis_index("tm")
    sp = lax.axis_index("space")
    y, core = tm // 2, tm % 2
    x, z = sp // SIDE, sp % SIDE
    late = y == GROUP
    early = y < GROUP
    sibling = (tm + 1 - 2 * core, sp)

    def place(i, sign):
        a, b = i % SIDE, (i // SIDE) % SIDE
        dx, dz = (3 * b + 2 * a) % SIDE, (3 * a + 2 * b) % SIDE
        return lax.rem(x + SIDE + sign * dx, SIDE) * SIDE + lax.rem(z + SIDE + sign * dz, SIDE)

    def ring(s):
        return lax.rem(y + s, GROUP)

    def wait(ref, sem):
        pltpu.make_async_copy(ref, ref, sem).wait()

    def columns(head):
        return pl.ds(pl.multiple_of(head * DH, DH), DH)

    barrier = pltpu.get_barrier_semaphore()

    for dx in range(SIDE):
        for dz in range(SIDE):
            for dy in range(SIDE):
                if dx or dz or dy:
                    where = lax.rem(x + dx, SIDE) * SIDE + lax.rem(z + dz, SIDE)
                    pl.semaphore_signal(
                        barrier, inc=1, device_id=(2 * lax.rem(y + dy, SIDE) + core, where),
                        device_id_type=MESH,
                    )
    pl.semaphore_signal(barrier, inc=1, device_id=sibling, device_id_type=MESH)
    pl.semaphore_wait(barrier, PLANE * SIDE)

    lists = ((lists_in, lists_v, lists_s), (reach_in, reach_v, reach_s))
    for k, (src, dst, _) in enumerate(lists):
        for d in range(1, SIDE):
            pltpu.make_async_remote_copy(
                src, dst.at[y], m_send.at[k], m_recv.at[k],
                device_id=(2 * lax.rem(y + d, SIDE) + core, sp), device_id_type=MESH,
            ).start()
        pltpu.make_async_copy(src, dst.at[y], m_recv.at[k]).start()

    def send(kind, src, dst, send_sem, recv_sem, by_way=None):
        def one(i, carry):
            s = lax.rem(i, GROUP)
            where = place(i, 1)
            there = GROUP if kind == "late" else ring(s)
            head = GROUP * where + (s if kind == "late" else there)
            piece = src.at[:, :, columns(head)]
            mine = lax.rem(i, PLANE) == 0
            if kind == "early":
                mine = jnp.logical_and(mine, s == 0)
            turn = jnp.logical_and(y == 0, s == 2) if by_way else False

            @pl.when(mine)
            def _():
                pltpu.make_async_copy(piece, dst(i), recv_sem.at[i]).start()

            @pl.when(jnp.logical_not(jnp.logical_or(mine, turn)))
            def _():
                pltpu.make_async_remote_copy(
                    piece, dst(i), send_sem, recv_sem.at[i],
                    device_id=(2 * there + core, where), device_id_type=MESH,
                ).start()

            if by_way:
                pass_buf, pass_recv = by_way

                @pl.when(turn)
                def _():
                    n = i // GROUP
                    pltpu.make_async_remote_copy(
                        piece, pass_buf.at[n], send_sem, pass_recv.at[n],
                        device_id=(2 * GROUP + core, where // SIDE * SIDE + z),
                        device_id_type=MESH,
                    ).start()

            return carry

        lax.fori_loop(0, PIECES, one, 0)

    def span_slot(buf, pair, j):
        return buf.at[pl.ds(2 * pair, 2), 2 * j + core]

    def swap(i, j, buf, recv, f_send, f_recv):
        piece = span_slot(buf, place(i, -1), j)
        wait(piece, recv.at[i])
        pltpu.make_async_remote_copy(
            piece, piece, f_send, f_recv, device_id=sibling, device_id_type=MESH
        ).start()

    def onward(n, pass_buf, pass_send, pass_recv, dst, recv):
        i = GROUP * n + 2
        wait(pass_buf.at[n], pass_recv.at[n])
        pltpu.make_async_remote_copy(
            pass_buf.at[n], dst(i), pass_send, recv.at[i],
            device_id=(2 * 2 + core, x * SIDE + place(i, 1) % SIDE), device_id_type=MESH,
        ).start()

    def from_zero(buf):
        return lambda i: span_slot(buf, place(i, -1) // SIDE * SIDE + z, 0)

    swap_k = (kbuf, k_recv, fk_send, fk_recv)
    swap_v = (vbuf, v_recv, fv_send, fv_recv)
    pass_k = (kpass, kp_send, kp_recv, from_zero(kbuf), k_recv)
    pass_q = (qpass, qp_send, qp_recv, lambda i: qbuf.at[i], q_recv)

    def lists_ready():
        for k, (_, buf, _) in enumerate(lists):
            wait(buf, m_recv.at[k])
        moves = [pltpu.make_async_copy(v, s, m_copy.at[k]) for k, (_, v, s) in enumerate(lists)]
        for move in moves:
            move.start()
        for move in moves:
            move.wait()

    def swapped():
        wait(kbuf.at[:, pl.ds(0, GROUP)], fk_recv)
        wait(vbuf.at[:, pl.ds(0, GROUP)], fv_recv)

    @pl.when(early)
    def _():
        send("early", k_in, lambda i: span_slot(kbuf, sp, y), k_send, k_recv, (kpass, kp_recv))
        send("early", v_in, lambda i: span_slot(vbuf, sp, y), v_send, v_recv)
        send("early", q_in, lambda i: qbuf.at[i], q_send, q_recv, (qpass, qp_recv))
        lists_ready()
        for what in (swap_k, swap_v):
            def pieces(i, carry):
                swap(i, lax.rem(y + GROUP - lax.rem(i, GROUP), GROUP), *what)
                return carry

            lax.fori_loop(0, PIECES, pieces, 0)
        swapped()

    @pl.when(late)
    def _():
        send("late", q_in, lambda i: qbuf.at[i], q_send, q_recv)
        send("late", k_in, lambda i: span_slot(kbuf, sp, lax.rem(i, GROUP)), k_send, k_recv)
        send("late", v_in, lambda i: span_slot(vbuf, sp, lax.rem(i, GROUP)), v_send, v_recv)
        lists_ready()

        def first(n, carry):
            onward(n, *pass_k)
            for h in range(GROUP):
                i = GROUP * n + h
                wait(qbuf.at[i], q_recv.at[i])
                pltpu.make_async_remote_copy(
                    qbuf.at[i], qbuf.at[PIECES + n], fq_send, q_recv.at[PIECES + n],
                    device_id=(2 * h + core, sp), device_id_type=MESH,
                ).start()
            return carry

        lax.fori_loop(0, PLANE, first, 0)

        def third(i, carry):
            swap(i, lax.rem(i, GROUP), *swap_k)
            return carry

        lax.fori_loop(0, PIECES, third, 0)

        def fourth(n, carry):
            onward(n, *pass_q)
            return carry

        lax.fori_loop(0, PLANE, fourth, 0)

        def fifth(i, carry):
            swap(i, lax.rem(i, GROUP), *swap_v)
            return carry

        lax.fori_loop(0, PIECES, fifth, 0)
        swapped()

    def attend(tasks):
        def rows(buf, t, other, first, width):
            spans, keys = pl.ds(first, width), width * TILE
            return jnp.concatenate(
                [buf[t, spans].reshape(keys, DH), buf[other, spans].reshape(keys, DH)], axis=0
            )

        scores = []
        for q, t, other, first, width, valid in tasks:
            bias = jnp.where(valid, 0.0, NEG)
            s = lax.dot_general(
                q, rows(kbuf, t, other, first, width), NT, preferred_element_type=jnp.float32
            )
            scores.append(s + jnp.concatenate([bias, bias], axis=1))
        tops = [jnp.max(s, axis=1, keepdims=True) for s in scores]
        weights = [jnp.exp2((s - top) * SCALE) for s, top in zip(scores, tops)]
        totals = [jnp.sum(e, axis=1, keepdims=True) for e in weights]
        sums = []
        for e, (_, t, other, first, width, _) in zip(weights, tasks):
            v = rows(vbuf, t, other, first, width)
            sums.append(jnp.dot(e.astype(jnp.bfloat16), v, preferred_element_type=jnp.float32))
        return [
            (r / total, lambda top=top, total=total: top * SCALE + jnp.log2(total))
            for r, top, total in zip(sums, tops, totals)
        ]

    def spans_of(width, first):
        return first + lax.broadcasted_iota(jnp.int32, (1, width * TILE), 1) // TILE

    def diagonal(half):
        shape = (TILE, DH)
        row = lax.broadcasted_iota(jnp.int32, shape, 0)
        lane = lax.broadcasted_iota(jnp.int32, shape, 1)
        return jnp.where(lane == row + half * TILE, 1.0, 0.0)

    @pl.when(early)
    def _():
        home = out.at[:, :, columns(GROUP * sp + y)]

        def task(i, half, j, pair):
            width = min(2 * (j + 1), 2 * GROUP)
            span = spans_of(width, 0)
            t = 2 * pair + half
            valid = span >= reach_s[j, 0, t]
            if j < GROUP:
                valid = jnp.logical_and(valid, span <= 2 * j + core)
            return qbuf[i, half], t, lists_s[j, 1, t], 0, width, valid

        def last_spans(m, carry):
            chunks = [BATCH * m + c for c in range(BATCH)]
            for n in chunks:
                wait(qbuf.at[PIECES + n], q_recv.at[PIECES + n])
            done = attend([
                task(PIECES + n, half, GROUP, place(GROUP * n + y, -1))
                for n in chunks for half in range(2)
            ])
            for c, n in enumerate(chunks):
                log = 0.0
                for half in range(2):
                    o, logs = done[2 * c + half]
                    obuf[PIECES + n, half] = o.astype(jnp.bfloat16)
                    log = log + jnp.sum(logs() * diagonal(half), axis=0, keepdims=True)
                lbuf[n] = jnp.broadcast_to(log, (8, DH))
            for n in chunks:
                piece = GROUP * n + y
                above = dict(device_id=(2 * GROUP + core, sp), device_id_type=MESH)
                pltpu.make_async_remote_copy(
                    obuf.at[PIECES + n], pbuf.at[piece], p_send, p_recv.at[piece], **above
                ).start()
                pltpu.make_async_remote_copy(
                    lbuf.at[n], plog.at[piece], l_send, l_recv.at[piece], **above
                ).start()
            return carry

        def work(m, carry):
            items = []
            for n in [STEP * m + c for c in range(STEP)]:
                for j in range(GROUP):
                    i = GROUP * n + lax.rem(y - j + GROUP, GROUP)
                    items.append((i, j, place(i, -1)))
            for i, _, _ in items:
                wait(qbuf.at[i], q_recv.at[i])
            done = attend([
                task(i, half, j, pair) for i, j, pair in items for half in range(2)
            ])
            for k, (i, j, pair) in enumerate(items):
                for half in range(2):
                    obuf[i, half] = done[2 * k + half][0].astype(jnp.bfloat16)
                mine = jnp.logical_and(lax.rem(i, PLANE) == 0, j == y)

                @pl.when(mine)
                def _():
                    pltpu.make_async_copy(obuf.at[i], home, o_recv).start()

                @pl.when(jnp.logical_not(mine))
                def _():
                    pltpu.make_async_remote_copy(
                        obuf.at[i], home, o_send, o_recv,
                        device_id=(2 * j + core, pair), device_id_type=MESH,
                    ).start()

            return carry

        def both(m, carry):
            last_spans(m + 1, 0)
            work(m, 0)
            return carry

        lax.fori_loop(0, 1, last_spans, 0)
        lax.fori_loop(0, PLANE // BATCH - 1, both, 0)
        lax.fori_loop(PLANE // BATCH - 1, PLANE // STEP, work, 0)
        wait(obuf.at[pl.ds(0, PIECES - 1)], o_send)
        wait(obuf.at[pl.ds(PIECES, PLANE)], p_send)
        wait(lbuf, l_send)

    @pl.when(late)
    def _():
        def work(n, carry):
            pieces = [GROUP * n + h for h in range(GROUP)]
            span = spans_of(2, 2 * GROUP)
            tasks = []
            for h, i in enumerate(pieces):
                pair = place(i, -1)
                for half in range(2):
                    t = 2 * pair + half
                    valid = jnp.logical_and(
                        span >= reach_s[GROUP, 0, t], span <= 2 * GROUP + core
                    )
                    tasks.append((qbuf[i, half], t, lists_s[GROUP, 1, t], 2 * h, 2, valid))
            done = attend(tasks)
            for i in pieces:
                wait(pbuf.at[i], p_recv.at[i])
                wait(plog.at[i], l_recv.at[i])
            merged = []
            for k, (o, log) in enumerate(done):
                i, half = pieces[k // 2], k % 2
                log_a = log()
                log_b = jnp.sum(plog[i, 0:1] * diagonal(half), axis=1, keepdims=True)
                big = jnp.maximum(log_a, log_b)
                factor_a = jnp.exp2(log_a - big)
                factor_b = jnp.exp2(log_b - big)
                numer = factor_a * o + factor_b * pbuf[i, half].astype(jnp.float32)
                merged.append((numer / (factor_a + factor_b)).astype(jnp.bfloat16))
            for k, o in enumerate(merged):
                obuf[pieces[k // 2], k % 2] = o
            for h, i in enumerate(pieces):
                home = out.at[:, :, columns(GROUP * sp + h)]
                mine = lax.rem(i, PLANE) == 0

                @pl.when(mine)
                def _():
                    pltpu.make_async_copy(obuf.at[i], home, o_recv).start()

                @pl.when(jnp.logical_not(mine))
                def _():
                    pltpu.make_async_remote_copy(
                        obuf.at[i], home, o_send, o_recv,
                        device_id=(2 * GROUP + core, place(i, -1)), device_id_type=MESH,
                    ).start()

            return carry

        lax.fori_loop(0, PLANE, work, 0)
        wait(obuf.at[pl.ds(0, PIECES - GROUP)], o_send)
        wait(qbuf.at[pl.ds(0, PIECES)], fq_send)
        wait(kpass, kp_send)
        wait(qpass, qp_send)

    wait(kbuf.at[:, pl.ds(0, GROUP)], fk_send)
    wait(vbuf.at[:, pl.ds(0, GROUP)], fv_send)
    for src, sem in ((q_in, q_send), (k_in, k_send), (v_in, v_send)):
        wait(src.at[:, :, pl.ds(0, (PIECES - GROUP) * DH)], sem)

        @pl.when(early)
        def _():
            wait(src.at[:, :, pl.ds(0, (GROUP - 1) * DH)], sem)

    for k, (_, buf, _) in enumerate(lists):
        wait(buf.at[pl.ds(0, SIDE - 1)], m_send.at[k])
    wait(out, o_recv)


def body(queries, key_rows, value_rows, tile_lists, span_reach):
    rows, width = queries.shape
    halves = (rows // TILE, TILE, width)
    dma = pltpu.SemaphoreType.DMA
    flops = 2 * 2 * 20 * TILES * TILE * 128 * DH
    out = pl.pallas_call(
        kernel,
        out_shape=jax.ShapeDtypeStruct(halves, queries.dtype),
        in_specs=[pl.BlockSpec(memory_space=pltpu.HBM)] * 3 + [pl.BlockSpec(memory_space=pl.ANY)] * 2,
        out_specs=pl.BlockSpec(memory_space=pl.ANY),
        scratch_shapes=[
            pltpu.VMEM((PIECES + PLANE, 2, TILE, DH), jnp.bfloat16),
            pltpu.VMEM((TILES, 2 * GROUP, TILE, DH), jnp.bfloat16),
            pltpu.VMEM((TILES, 2 * GROUP, TILE, DH), jnp.bfloat16),
            pltpu.VMEM((PIECES + PLANE, 2, TILE, DH), jnp.bfloat16),
            pltpu.VMEM((PLANE, 8, DH), jnp.float32),
            pltpu.VMEM((PIECES, 2, TILE, DH), jnp.bfloat16),
            pltpu.VMEM((PIECES, 8, DH), jnp.float32),
            pltpu.VMEM((PLANE, 2, TILE, DH), jnp.bfloat16),
            pltpu.VMEM((PLANE, 2, TILE, DH), jnp.bfloat16),
            pltpu.VMEM((SIDE, 2, TILES), jnp.int32),
            pltpu.VMEM((SIDE, 1, TILES), jnp.int32),
            pltpu.SMEM((SIDE, 2, TILES), jnp.int32),
            pltpu.SMEM((SIDE, 1, TILES), jnp.int32),
            dma, dma, dma, dma, dma, dma, dma((2,)),
            dma((PIECES + PLANE,)), dma((PIECES,)), dma((PIECES,)), dma,
            dma((PIECES,)), dma((PIECES,)), dma((2,)),
            dma, dma, dma, dma, dma, dma((2,)),
            dma, dma((PLANE,)), dma, dma((PLANE,)),
        ],
        compiler_params=pltpu.CompilerParams(
            collective_id=0, has_side_effects=True, vmem_limit_bytes=48 << 20
        ),
        cost_estimate=pl.CostEstimate(
            flops=flops, bytes_accessed=4 * rows * width * 2, transcendentals=flops // 512
        ),
        name="attend",
    )(
        *(
            pltpu.with_memory_space_constraint(array, pltpu.HBM)
            for array in (
                queries.reshape(halves), key_rows.reshape(halves), value_rows.reshape(halves),
                tile_lists[0].T, span_reach,
            )
        ),
    )
    return out.reshape(rows, width)


def solution(mesh):
    in_specs = (
        P(("tm", "space"), None),
        P(("tm", "space"), None),
        P(("tm", "space"), None),
        P("tm", None, None),
        P("tm", None),
    )
    return jax.shard_map(
        body, mesh=mesh, in_specs=in_specs, out_specs=P(("tm", "space"), None), check_vma=False
    )
```

```python
import math

import jax
import jax.numpy as jnp
from jax import lax
from jax.experimental import pallas as pl
from jax.experimental.pallas import tpu as pltpu
from jax.sharding import PartitionSpec as P

MESH = pl.DeviceIdType.MESH
DH = 128
TILE = 64
SIDE = 4
PLANE = SIDE * SIDE
HEADS = 48
GROUP = 3
TILES = 32
PIECES = PLANE * GROUP
BATCH = 2
STEP = 2
NEG = -1e30
SCALE = DH ** -0.5 * math.log2(math.e)
NT = (((1,), (1,)), ((), ()))


def kernel(
    q_in, k_in, v_in, lists_in, reach_in, out,
    qbuf, kbuf, vbuf, obuf, lbuf, pbuf, plog, kpass, qpass, lists_v, reach_v, lists_s, reach_s,
    q_send, k_send, v_send, o_send, p_send, l_send, m_send,
    q_recv, k_recv, v_recv, o_recv, p_recv, l_recv, m_recv,
    fk_send, fk_recv, fv_send, fv_recv, fq_send, m_copy, kp_send, kp_recv, qp_send, qp_recv,
):
    tm = lax.axis_index("tm")
    sp = lax.axis_index("space")
    y, core = tm // 2, tm % 2
    x, z = sp // SIDE, sp % SIDE
    late = y == GROUP
    early = y < GROUP
    sibling = (tm + 1 - 2 * core, sp)

    def place(i, sign):
        a, b = i % SIDE, (i // SIDE) % SIDE
        dx, dz = (3 * b + 2 * a) % SIDE, (3 * a + 2 * b) % SIDE
        return lax.rem(x + SIDE + sign * dx, SIDE) * SIDE + lax.rem(z + SIDE + sign * dz, SIDE)

    def ring(s):
        return lax.rem(y + s, GROUP)

    def wait(ref, sem):
        pltpu.make_async_copy(ref, ref, sem).wait()

    def columns(head):
        return pl.ds(pl.multiple_of(head * DH, DH), DH)

    barrier = pltpu.get_barrier_semaphore()

    for dx in range(SIDE):
        for dz in range(SIDE):
            for dy in range(SIDE):
                if dx or dz or dy:
                    where = lax.rem(x + dx, SIDE) * SIDE + lax.rem(z + dz, SIDE)
                    pl.semaphore_signal(
                        barrier, inc=1, device_id=(2 * lax.rem(y + dy, SIDE) + core, where),
                        device_id_type=MESH,
                    )
    pl.semaphore_signal(barrier, inc=1, device_id=sibling, device_id_type=MESH)
    pl.semaphore_wait(barrier, PLANE * SIDE)

    lists = ((lists_in, lists_v, lists_s), (reach_in, reach_v, reach_s))

    def send_lists():
        for k, (src, dst, _) in enumerate(lists):
            for d in range(1, SIDE):
                pltpu.make_async_remote_copy(
                    src, dst.at[y], m_send.at[k], m_recv.at[k],
                    device_id=(2 * lax.rem(y + d, SIDE) + core, sp), device_id_type=MESH,
                ).start()
            pltpu.make_async_copy(src, dst.at[y], m_recv.at[k]).start()

    def send(kind, src, dst, send_sem, recv_sem, by_way=None):
        def one(i, carry):
            s = lax.rem(i, GROUP)
            where = place(i, 1)
            there = GROUP if kind == "late" else ring(s)
            head = GROUP * where + (s if kind == "late" else there)
            piece = src.at[:, :, columns(head)]
            mine = lax.rem(i, PLANE) == 0
            if kind == "early":
                mine = jnp.logical_and(mine, s == 0)
            turn = jnp.logical_and(y == 0, s == 2) if by_way else False

            @pl.when(mine)
            def _():
                pltpu.make_async_copy(piece, dst(i), recv_sem.at[i]).start()

            @pl.when(jnp.logical_not(jnp.logical_or(mine, turn)))
            def _():
                pltpu.make_async_remote_copy(
                    piece, dst(i), send_sem, recv_sem.at[i],
                    device_id=(2 * there + core, where), device_id_type=MESH,
                ).start()

            if by_way:
                pass_buf, pass_recv = by_way

                @pl.when(turn)
                def _():
                    n = i // GROUP
                    pltpu.make_async_remote_copy(
                        piece, pass_buf.at[n], send_sem, pass_recv.at[n],
                        device_id=(2 * GROUP + core, where // SIDE * SIDE + z),
                        device_id_type=MESH,
                    ).start()

            return carry

        lax.fori_loop(0, PIECES, one, 0)

    def span_slot(buf, pair, j):
        return buf.at[pl.ds(2 * pair, 2), 2 * j + core]

    def swap(i, j, buf, recv, f_send, f_recv):
        piece = span_slot(buf, place(i, -1), j)
        wait(piece, recv.at[i])
        pltpu.make_async_remote_copy(
            piece, piece, f_send, f_recv, device_id=sibling, device_id_type=MESH
        ).start()

    def onward(n, pass_buf, pass_send, pass_recv, dst, recv):
        i = GROUP * n + 2
        wait(pass_buf.at[n], pass_recv.at[n])
        pltpu.make_async_remote_copy(
            pass_buf.at[n], dst(i), pass_send, recv.at[i],
            device_id=(2 * 2 + core, x * SIDE + place(i, 1) % SIDE), device_id_type=MESH,
        ).start()

    def from_zero(buf):
        return lambda i: span_slot(buf, place(i, -1) // SIDE * SIDE + z, 0)

    swap_k = (kbuf, k_recv, fk_send, fk_recv)
    swap_v = (vbuf, v_recv, fv_send, fv_recv)
    pass_k = (kpass, kp_send, kp_recv, from_zero(kbuf), k_recv)
    pass_q = (qpass, qp_send, qp_recv, lambda i: qbuf.at[i], q_recv)

    def lists_ready():
        for k, (_, buf, _) in enumerate(lists):
            wait(buf, m_recv.at[k])
        moves = [pltpu.make_async_copy(v, s, m_copy.at[k]) for k, (_, v, s) in enumerate(lists)]
        for move in moves:
            move.start()
        for move in moves:
            move.wait()

    def swapped():
        wait(kbuf.at[:, pl.ds(0, GROUP)], fk_recv)
        wait(vbuf.at[:, pl.ds(0, GROUP)], fv_recv)

    @pl.when(early)
    def _():
        send("early", k_in, lambda i: span_slot(kbuf, sp, y), k_send, k_recv, (kpass, kp_recv))
        send_lists()
        send("early", v_in, lambda i: span_slot(vbuf, sp, y), v_send, v_recv)
        send("early", q_in, lambda i: qbuf.at[i], q_send, q_recv, (qpass, qp_recv))
        lists_ready()
        for what in (swap_k, swap_v):
            def pieces(i, carry):
                swap(i, lax.rem(y + GROUP - lax.rem(i, GROUP), GROUP), *what)
                return carry

            lax.fori_loop(0, PIECES, pieces, 0)
        swapped()

    @pl.when(late)
    def _():
        send("late", q_in, lambda i: qbuf.at[i], q_send, q_recv)
        send("late", k_in, lambda i: span_slot(kbuf, sp, lax.rem(i, GROUP)), k_send, k_recv)
        send_lists()
        send("late", v_in, lambda i: span_slot(vbuf, sp, lax.rem(i, GROUP)), v_send, v_recv)
        lists_ready()

        def first(n, carry):
            onward(n, *pass_k)
            for h in range(GROUP):
                i = GROUP * n + h
                wait(qbuf.at[i], q_recv.at[i])
                pltpu.make_async_remote_copy(
                    qbuf.at[i], qbuf.at[PIECES + n], fq_send, q_recv.at[PIECES + n],
                    device_id=(2 * h + core, sp), device_id_type=MESH,
                ).start()
            return carry

        lax.fori_loop(0, PLANE, first, 0)

        def third(i, carry):
            swap(i, lax.rem(i, GROUP), *swap_k)
            return carry

        lax.fori_loop(0, PIECES, third, 0)

        def fourth(n, carry):
            onward(n, *pass_q)
            return carry

        lax.fori_loop(0, PLANE, fourth, 0)

        def fifth(i, carry):
            swap(i, lax.rem(i, GROUP), *swap_v)
            return carry

        lax.fori_loop(0, PIECES, fifth, 0)
        swapped()

    def attend(tasks):
        def rows(buf, t, other, first, width):
            spans, keys = pl.ds(first, width), width * TILE
            return jnp.concatenate(
                [buf[t, spans].reshape(keys, DH), buf[other, spans].reshape(keys, DH)], axis=0
            )

        scores = []
        for q, t, other, first, width, valid in tasks:
            bias = jnp.where(valid, 0.0, NEG)
            s = lax.dot_general(
                q, rows(kbuf, t, other, first, width), NT, preferred_element_type=jnp.float32
            )
            scores.append(s + jnp.concatenate([bias, bias], axis=1))
        tops = [jnp.max(s, axis=1, keepdims=True) for s in scores]
        weights = [jnp.exp2((s - top) * SCALE) for s, top in zip(scores, tops)]
        totals = [jnp.sum(e, axis=1, keepdims=True) for e in weights]
        sums = []
        for e, (_, t, other, first, width, _) in zip(weights, tasks):
            v = rows(vbuf, t, other, first, width)
            sums.append(jnp.dot(e.astype(jnp.bfloat16), v, preferred_element_type=jnp.float32))
        return [
            (r / total, lambda top=top, total=total: top * SCALE + jnp.log2(total))
            for r, top, total in zip(sums, tops, totals)
        ]

    def spans_of(width, first):
        return first + lax.broadcasted_iota(jnp.int32, (1, width * TILE), 1) // TILE

    def diagonal(half):
        shape = (TILE, DH)
        row = lax.broadcasted_iota(jnp.int32, shape, 0)
        lane = lax.broadcasted_iota(jnp.int32, shape, 1)
        return jnp.where(lane == row + half * TILE, 1.0, 0.0)

    @pl.when(early)
    def _():
        home = out.at[:, :, columns(GROUP * sp + y)]

        def task(i, half, j, pair):
            width = min(2 * (j + 1), 2 * GROUP)
            span = spans_of(width, 0)
            t = 2 * pair + half
            valid = span >= reach_s[j, 0, t]
            if j < GROUP:
                valid = jnp.logical_and(valid, span <= 2 * j + core)
            return qbuf[i, half], t, lists_s[j, 1, t], 0, width, valid

        def last_spans(m, carry):
            chunks = [BATCH * m + c for c in range(BATCH)]
            for n in chunks:
                wait(qbuf.at[PIECES + n], q_recv.at[PIECES + n])
            done = attend([
                task(PIECES + n, half, GROUP, place(GROUP * n + y, -1))
                for n in chunks for half in range(2)
            ])
            for c, n in enumerate(chunks):
                log = 0.0
                for half in range(2):
                    o, logs = done[2 * c + half]
                    obuf[PIECES + n, half] = o.astype(jnp.bfloat16)
                    log = log + jnp.sum(logs() * diagonal(half), axis=0, keepdims=True)
                lbuf[n] = jnp.broadcast_to(log, (8, DH))
            for n in chunks:
                piece = GROUP * n + y
                above = dict(device_id=(2 * GROUP + core, sp), device_id_type=MESH)
                pltpu.make_async_remote_copy(
                    obuf.at[PIECES + n], pbuf.at[piece], p_send, p_recv.at[piece], **above
                ).start()
                pltpu.make_async_remote_copy(
                    lbuf.at[n], plog.at[piece], l_send, l_recv.at[piece], **above
                ).start()
            return carry

        def work(m, carry):
            items = []
            for n in [STEP * m + c for c in range(STEP)]:
                for j in range(GROUP):
                    i = GROUP * n + lax.rem(y - j + GROUP, GROUP)
                    items.append((i, j, place(i, -1)))
            for i, _, _ in items:
                wait(qbuf.at[i], q_recv.at[i])
            done = attend([
                task(i, half, j, pair) for i, j, pair in items for half in range(2)
            ])
            for k, (i, j, pair) in enumerate(items):
                for half in range(2):
                    obuf[i, half] = done[2 * k + half][0].astype(jnp.bfloat16)
                mine = jnp.logical_and(lax.rem(i, PLANE) == 0, j == y)

                @pl.when(mine)
                def _():
                    pltpu.make_async_copy(obuf.at[i], home, o_recv).start()

                @pl.when(jnp.logical_not(mine))
                def _():
                    pltpu.make_async_remote_copy(
                        obuf.at[i], home, o_send, o_recv,
                        device_id=(2 * j + core, pair), device_id_type=MESH,
                    ).start()

            return carry

        def both(m, carry):
            last_spans(m + 1, 0)
            work(m, 0)
            return carry

        lax.fori_loop(0, 1, last_spans, 0)
        lax.fori_loop(0, PLANE // BATCH - 1, both, 0)
        lax.fori_loop(PLANE // BATCH - 1, PLANE // STEP, work, 0)
        wait(obuf.at[pl.ds(0, PIECES - 1)], o_send)
        wait(obuf.at[pl.ds(PIECES, PLANE)], p_send)
        wait(lbuf, l_send)

    @pl.when(late)
    def _():
        def work(n, carry):
            pieces = [GROUP * n + h for h in range(GROUP)]
            span = spans_of(2, 2 * GROUP)
            tasks = []
            for h, i in enumerate(pieces):
                pair = place(i, -1)
                for half in range(2):
                    t = 2 * pair + half
                    valid = jnp.logical_and(
                        span >= reach_s[GROUP, 0, t], span <= 2 * GROUP + core
                    )
                    tasks.append((qbuf[i, half], t, lists_s[GROUP, 1, t], 2 * h, 2, valid))
            done = attend(tasks)
            for i in pieces:
                wait(pbuf.at[i], p_recv.at[i])
                wait(plog.at[i], l_recv.at[i])
            merged = []
            for k, (o, log) in enumerate(done):
                i, half = pieces[k // 2], k % 2
                log_a = log()
                log_b = jnp.sum(plog[i, 0:1] * diagonal(half), axis=1, keepdims=True)
                big = jnp.maximum(log_a, log_b)
                factor_a = jnp.exp2(log_a - big)
                factor_b = jnp.exp2(log_b - big)
                numer = factor_a * o + factor_b * pbuf[i, half].astype(jnp.float32)
                merged.append((numer / (factor_a + factor_b)).astype(jnp.bfloat16))
            for k, o in enumerate(merged):
                obuf[pieces[k // 2], k % 2] = o
            for h, i in enumerate(pieces):
                home = out.at[:, :, columns(GROUP * sp + h)]
                mine = lax.rem(i, PLANE) == 0

                @pl.when(mine)
                def _():
                    pltpu.make_async_copy(obuf.at[i], home, o_recv).start()

                @pl.when(jnp.logical_not(mine))
                def _():
                    pltpu.make_async_remote_copy(
                        obuf.at[i], home, o_send, o_recv,
                        device_id=(2 * GROUP + core, place(i, -1)), device_id_type=MESH,
                    ).start()

            return carry

        lax.fori_loop(0, PLANE, work, 0)
        wait(obuf.at[pl.ds(0, PIECES - GROUP)], o_send)
        wait(qbuf.at[pl.ds(0, PIECES)], fq_send)
        wait(kpass, kp_send)
        wait(qpass, qp_send)

    wait(kbuf.at[:, pl.ds(0, GROUP)], fk_send)
    wait(vbuf.at[:, pl.ds(0, GROUP)], fv_send)
    for src, sem in ((q_in, q_send), (k_in, k_send), (v_in, v_send)):
        wait(src.at[:, :, pl.ds(0, (PIECES - GROUP) * DH)], sem)

        @pl.when(early)
        def _():
            wait(src.at[:, :, pl.ds(0, (GROUP - 1) * DH)], sem)

    for k, (_, buf, _) in enumerate(lists):
        wait(buf.at[pl.ds(0, SIDE - 1)], m_send.at[k])
    wait(out, o_recv)


def body(queries, key_rows, value_rows, tile_lists, span_reach):
    rows, width = queries.shape
    halves = (rows // TILE, TILE, width)
    dma = pltpu.SemaphoreType.DMA
    flops = 2 * 2 * 20 * TILES * TILE * 128 * DH
    out = pl.pallas_call(
        kernel,
        out_shape=jax.ShapeDtypeStruct(halves, queries.dtype),
        in_specs=[pl.BlockSpec(memory_space=pltpu.HBM)] * 3 + [pl.BlockSpec(memory_space=pl.ANY)] * 2,
        out_specs=pl.BlockSpec(memory_space=pl.ANY),
        scratch_shapes=[
            pltpu.VMEM((PIECES + PLANE, 2, TILE, DH), jnp.bfloat16),
            pltpu.VMEM((TILES, 2 * GROUP, TILE, DH), jnp.bfloat16),
            pltpu.VMEM((TILES, 2 * GROUP, TILE, DH), jnp.bfloat16),
            pltpu.VMEM((PIECES + PLANE, 2, TILE, DH), jnp.bfloat16),
            pltpu.VMEM((PLANE, 8, DH), jnp.float32),
            pltpu.VMEM((PIECES, 2, TILE, DH), jnp.bfloat16),
            pltpu.VMEM((PIECES, 8, DH), jnp.float32),
            pltpu.VMEM((PLANE, 2, TILE, DH), jnp.bfloat16),
            pltpu.VMEM((PLANE, 2, TILE, DH), jnp.bfloat16),
            pltpu.VMEM((SIDE, 2, TILES), jnp.int32),
            pltpu.VMEM((SIDE, 1, TILES), jnp.int32),
            pltpu.SMEM((SIDE, 2, TILES), jnp.int32),
            pltpu.SMEM((SIDE, 1, TILES), jnp.int32),
            dma, dma, dma, dma, dma, dma, dma((2,)),
            dma((PIECES + PLANE,)), dma((PIECES,)), dma((PIECES,)), dma,
            dma((PIECES,)), dma((PIECES,)), dma((2,)),
            dma, dma, dma, dma, dma, dma((2,)),
            dma, dma((PLANE,)), dma, dma((PLANE,)),
        ],
        compiler_params=pltpu.CompilerParams(
            collective_id=0, has_side_effects=True, vmem_limit_bytes=48 << 20
        ),
        cost_estimate=pl.CostEstimate(
            flops=flops, bytes_accessed=4 * rows * width * 2, transcendentals=flops // 512
        ),
        name="attend",
    )(
        *(
            pltpu.with_memory_space_constraint(array, pltpu.HBM)
            for array in (
                queries.reshape(halves), key_rows.reshape(halves), value_rows.reshape(halves),
                tile_lists[0].T, span_reach,
            )
        ),
    )
    return out.reshape(rows, width)


def solution(mesh):
    in_specs = (
        P(("tm", "space"), None),
        P(("tm", "space"), None),
        P(("tm", "space"), None),
        P("tm", None, None),
        P("tm", None),
    )
    return jax.shard_map(
        body, mesh=mesh, in_specs=in_specs, out_specs=P(("tm", "space"), None), check_vma=False
    )
```
